256 devices in a mesh: dp: 64 (over x, z_hi, y, core), group: 4 (over z_lo).
Axes of the slice: x: 4, y: 4, z: 8 (z_hi: 2, z_lo: 4; z = z_hi * 4 + z_lo), core: 2. Of those that a mesh axis runs over, the one named last changes fastest.
Arguments:
- activations: bfloat16 [65536, 4096], P('dp', 'group'), may hold values from -36 to 36
- output_grads: bfloat16 [65536, 8192], P(('dp', 'group')), may hold values from -36 to 36
- token_counts: int32 [64], replicated, may hold values from 513 to 1024, as said below
- owner_blocks: int32 [64], replicated, may hold values from 0 to 63, each once
- basis_in: bfloat16 [4, 1024, 1024], P('group', 'dp'), may hold values from -0.1875 to 0.1875
- basis_out: bfloat16 [64, 128, 128], P('dp'), may hold values from -0.5 to 0.5
- values_in: float32 [4096], P('group'), may hold values from 0.1 to 1
- values_out: float32 [8192], P('dp'), may hold values from 0.1 to 1
- gradient: bfloat16 [4096, 8192], P('group', 'dp'), may hold values from -3500 to 3500
- learning_rate: float32 [1], replicated, may hold values from 3e-06 to 1.2e-05
Outputs:
- cov_in: float32 [4, 1024, 1024], P('group', 'dp')
- cov_out: float32 [64, 128, 128], P('dp', 'group')
- update: float32 [4096, 8192], P('group', 'dp')
The draws below stay inside these ranges and needn't reach their ends.
Inputs may be any that keep to these rules, and one draw needn't show every extreme that they name: `token_counts`: each shard counts at least half of its 1024 tokens; some shard counts all of them and some shard exactly 513. `owner_blocks`: each block number appears once.
All inputs are finite; a program needn't handle non-finite values.
Results may differ from the reference program's by a relative error of at most 0.0026.
The reference program's roundings to bfloat16 on the way (of `in_masked`, `out_masked`, `rotated`, `scaled` and `back_rot`) count: a program that leaves them out, or rounds other values in their place, can miss the bound.
Values may be sent and summed in bfloat16 or wider, within the bound.
No kernel may reach another device: no remote copies, remote signals or barrier semaphores. Data moves between devices by JAX's collectives and lax.ppermute only.
A program may use at most 64 MiB of HBM per device.

```python
import math
import jax
import jax.numpy as jnp
from jax import lax

D = 4096
BG = 128
TOK_DEV = 1024
BA = 1024
FW = 8192
TOKENS = 65536
N_DP = 64


def scaled_rows(key, rows, cols, lo, hi):
    key_rows, key_cols = jax.random.split(key)
    row_scale = jnp.exp(jax.random.uniform(key_rows, (rows, 1), jnp.float32, math.log(lo), math.log(hi)))
    col_scale = jnp.exp(jax.random.uniform(key_cols, (1, cols), jnp.float32, math.log(lo), math.log(hi)))
    return (row_scale, col_scale)


def draw_activations(key, part):
    key = jax.random.fold_in(key, 11)
    key_base, key_scale = jax.random.split(key, 2)
    row_scale, col_scale = scaled_rows(key_scale, TOKENS, D, 0.3, 3.0)
    base = jax.random.truncated_normal(key_base, -4.0, 4.0, (TOKENS, D), jnp.float32)
    return (base * row_scale * col_scale).astype(jnp.bfloat16)


def draw_output_grads(key, part):
    key = jax.random.fold_in(key, 23)
    key_base, key_scale = jax.random.split(key, 2)
    row_scale, col_scale = scaled_rows(key_scale, TOKENS, FW, 0.3, 3.0)
    base = jax.random.truncated_normal(key_base, -4.0, 4.0, (TOKENS, FW), jnp.float32)
    return (base * row_scale * col_scale).astype(jnp.bfloat16)


def draw_gradient(key, part):
    key = jax.random.fold_in(key, 37)
    key_base, key_scale = jax.random.split(key)
    row_scale, col_scale = scaled_rows(key_scale, D, FW, 1.0, 10.0)
    column = jnp.arange(FW, dtype=jnp.float32)[None, :] / FW
    base = jax.random.truncated_normal(key_base, -4.0, 4.0, (D, FW), jnp.float32)
    rising = jnp.exp(column * math.log(3.0) * 0.5)
    return (2.0 * base * row_scale * col_scale * rising).astype(jnp.bfloat16)


def draw_token_counts(key, part):
    key = jax.random.fold_in(key, 53)
    key_drop, key_full, key_half = jax.random.split(key, 3)
    counts = TOK_DEV - jax.random.randint(key_drop, (N_DP,), 0, TOK_DEV // 2)
    full_at = jax.random.randint(key_full, (), 0, N_DP)
    half_at = (full_at + 1 + jax.random.randint(key_half, (), 0, N_DP - 1)) % N_DP
    slots = jnp.arange(N_DP, dtype=jnp.int32)
    counts = jnp.where(slots == full_at, TOK_DEV, counts)
    counts = jnp.where(slots == half_at, TOK_DEV // 2 + 1, counts)
    return counts.astype(jnp.int32)


def steps_of(key, shape, cuts, least, largest):
    gain = 1.0
    for axis_at, blocks in cuts:
        steps = jax.random.uniform(jax.random.fold_in(jax.random.fold_in(key, 6), axis_at), (blocks,), jnp.float32, least / len(cuts), largest / len(cuts))
        gain = gain * jnp.repeat(jnp.exp(steps), shape[axis_at] // blocks).reshape((-1,) + (1,) * (len(shape) - 1 - axis_at))
    return gain


def bell_draw(own_key, shape, width, limit, shards=(), kind=jnp.bfloat16):
    level = steps_of(own_key, shape, shards, -0.22, 0.18) if shards else 1.0
    values = jax.random.normal(own_key, shape, jnp.float32) * width * level
    return jnp.minimum(jnp.maximum(values, -limit), limit).astype(kind)


def setup_inputs(seed: int = 0) -> dict:
    arg_keys = jax.random.split(jax.random.key(seed), 11)
    activations = draw_activations(jax.random.fold_in(arg_keys[10], 71), 0)
    output_grads = draw_output_grads(jax.random.fold_in(arg_keys[10], 71), 0)
    token_counts = draw_token_counts(jax.random.fold_in(arg_keys[10], 71), 0)
    owner_blocks = jax.random.permutation(arg_keys[3], N_DP).astype(jnp.int32)
    basis_in = bell_draw(arg_keys[4], (D // BA, BA, BA), BA ** -0.5, 0.1875, ((0, 4), (1, 64)))
    basis_out = bell_draw(arg_keys[5], (N_DP, BG, BG), BG ** -0.5, 0.5, ((0, 64),))
    values_in = jnp.clip(jnp.exp(math.log(1.0) - 2.3025851 * jax.random.uniform(arg_keys[6], (D,), jnp.float32) ** steps_of(arg_keys[6], (D,), ((0, 4),), -0.2, 0.2)), 0.1, 1.0)
    values_out = jnp.clip(jnp.exp(math.log(1.0) - 2.3025851 * jax.random.uniform(arg_keys[7], (FW,), jnp.float32) ** steps_of(arg_keys[7], (FW,), ((0, 64),), -0.2, 0.2)), 0.1, 1.0)
    gradient = draw_gradient(jax.random.fold_in(arg_keys[10], 71), 0)
    learning_rate = jnp.clip(jnp.exp(jax.random.uniform(arg_keys[9], (1,), jnp.float32, math.log(3.000000106112566e-06), math.log(1.2000000424450263e-05))), 3.000000106112566e-06, 1.2000000424450263e-05)
    return dict(activations=activations, output_grads=output_grads, token_counts=token_counts, owner_blocks=owner_blocks, basis_in=basis_in, basis_out=basis_out, values_in=values_in, values_out=values_out, gradient=gradient, learning_rate=learning_rate)


damping = 0.03
kl_clip = 0.001

def reference(activations, output_grads, token_counts, owner_blocks, basis_in, basis_out, values_in, values_out, gradient, learning_rate):
    token_total = jnp.sum(token_counts).astype(jnp.float32)
    position = jnp.arange(TOKENS, dtype=jnp.int32)
    shard_of = position // TOK_DEV
    counted = position % TOK_DEV < jnp.take(token_counts, shard_of)
    in_masked = jnp.where(counted[:, None], activations, jnp.zeros((), jnp.bfloat16))
    out_masked = jnp.where(counted[:, None], output_grads, jnp.zeros((), jnp.bfloat16))

    def in_block(index):
        cols = lax.dynamic_slice_in_dim(in_masked, (index * BA).astype(jnp.int32), BA, 1)
        return jnp.dot(cols.T, cols, preferred_element_type=jnp.float32) / token_total
    cov_in = lax.map(in_block, jnp.arange(D // BA, dtype=jnp.int32))

    def out_block(index):
        cols = lax.dynamic_slice_in_dim(out_masked, (index * BG).astype(jnp.int32), BG, 1)
        return jnp.dot(cols.T, cols, preferred_element_type=jnp.float32) / token_total
    cov_out = lax.map(out_block, owner_blocks.astype(jnp.int32))
    basis_f = basis_out.astype(jnp.float32)
    eig_out = values_out.reshape(N_DP, BG)
    pieces = []
    inner = jnp.zeros((), jnp.float32)
    for block in range(D // BA):
        grad_rows = gradient[block * BA:(block + 1) * BA]
        q_in = basis_in[block]
        rotated = jnp.dot(q_in.T, grad_rows, preferred_element_type=jnp.float32).astype(jnp.bfloat16)
        spectral = jnp.einsum('kbc,bcj->kbj', rotated.reshape(BA, N_DP, BG).astype(jnp.float32), basis_f)
        denom = values_in[block * BA:(block + 1) * BA][:, None, None] * eig_out[None, :, :] + damping
        scaled = (spectral / denom).astype(jnp.bfloat16)
        back_rot = jnp.einsum('kbc,bjc->kbj', scaled.astype(jnp.float32), basis_f).astype(jnp.bfloat16)
        precond = jnp.dot(q_in, back_rot.reshape(BA, FW), preferred_element_type=jnp.float32)
        inner = inner + jnp.sum(precond * grad_rows.astype(jnp.float32))
        pieces.append(precond)
    precond_all = jnp.concatenate(pieces, axis=0)
    clip_factor = jnp.minimum(1.0, jnp.sqrt(kl_clip / (learning_rate[0] * learning_rate[0] * inner)))
    update = clip_factor * precond_all
    return (cov_in, cov_out, update)
```

```python
import jax
import jax.numpy as jnp
from jax import lax
from jax.experimental import pallas as pl
from jax.experimental.pallas import tpu as pltpu
from jax.sharding import Mesh, PartitionSpec as P

damping = 0.03
kl_clip = 0.001
f32 = jnp.float32
bf16 = jnp.bfloat16

AXES = ("x", "zh", "y", "core", "zl")
SIZES = (4, 2, 4, 2, 4)
DP = ("x", "zh", "y", "core")
PLANE = ("x", "y")
COLUMN = ("zh", "zl")
VMEM = 40 << 20

ROWS_IN = 256
ROWS_OUT = 128
ROWS_EXTRA = 16
ROWS = ROWS_IN + ROWS_OUT + ROWS_EXTRA


def dot(a, b, ca, cb):
    return lax.dot_general(a, b, (((ca,), (cb,)), ((), ())), preferred_element_type=f32)


def cov_out_kernel(owners, meta, *refs):
    blocks, (send, keep) = refs[:8], refs[8:]
    live = meta[1]
    rows = lax.broadcasted_iota(jnp.int32, blocks[0].shape, 0) < live
    for y in range(4):
        for src, dst in ((blocks[y], keep), (blocks[4 + y], send)):
            full = src[...]
            masked = jnp.where(rows, full, jnp.zeros((), bf16))
            dst[y] = dot(masked, full, 0, 0)


def cov_out_partial(output_grads, owners, meta):
    quarter = output_grads.shape[0]

    def at(y, other):
        def index(s, owners, meta):
            core = 1 - meta[0] if other else meta[0]
            return (0, owners[(s * 4 + y) * 2 + core])

        return pl.BlockSpec((quarter, 128), index)

    out = pl.BlockSpec((4, 128, 128), lambda s, owners, meta: (s, 0, 0))
    return pl.pallas_call(
        cov_out_kernel,
        grid_spec=pltpu.PrefetchScalarGridSpec(
            num_scalar_prefetch=2,
            grid=(8,),
            in_specs=[at(y, False) for y in range(4)] + [at(y, True) for y in range(4)],
            out_specs=[out, out],
        ),
        out_shape=[jax.ShapeDtypeStruct((32, 128, 128), f32)] * 2,
        compiler_params=pltpu.CompilerParams(vmem_limit_bytes=VMEM),
        cost_estimate=pl.CostEstimate(
            flops=2 * quarter * 8192 * 128, bytes_accessed=quarter * 8192 * 2 + (4 << 20), transcendentals=0
        ),
        name="cov_out_partial",
    )(owners, meta, *([output_grads] * 8))


def cov_in_kernel(meta, lhs, rhs, send, keep):
    first = meta[0] == 0
    rows = lax.broadcasted_iota(jnp.int32, lhs.shape, 0) < meta[2]
    masked = jnp.where(rows, lhs[...], jnp.zeros((), bf16))
    part = dot(masked, rhs[...], 0, 0).reshape(8, 2, 16, 1024)
    keep[...] = jnp.where(first, part[:, 0], part[:, 1])
    send[...] = jnp.where(first, part[:, 1], part[:, 0])


def cov_in_partial(activations, meta):
    tok = activations.shape[0]
    out = pl.BlockSpec((8, 16, 1024), lambda s, meta: (s, 0, 0))
    return pl.pallas_call(
        cov_in_kernel,
        grid_spec=pltpu.PrefetchScalarGridSpec(
            num_scalar_prefetch=1,
            grid=(4,),
            in_specs=[
                pl.BlockSpec((tok, 256), lambda s, meta: (0, s)),
                pl.BlockSpec((tok, 1024), lambda s, meta: (0, 0)),
            ],
            out_specs=[out, out],
        ),
        out_shape=[jax.ShapeDtypeStruct((32, 16, 1024), f32)] * 2,
        compiler_params=pltpu.CompilerParams(vmem_limit_bytes=VMEM),
        cost_estimate=pl.CostEstimate(
            flops=2 * tok * 1024 * 1024, bytes_accessed=tok * 4096 + (4 << 20), transcendentals=0
        ),
        name="cov_in_partial",
    )(meta, activations, activations)


def pack_kernel(keep_out, recv_out, keep_in, recv_in, msg):
    row = lax.broadcasted_iota(jnp.int32, (128, 128), 0)
    col = lax.broadcasted_iota(jnp.int32, (128, 128), 1)
    for y in range(4):
        first = keep_out[0, y] + recv_out[0, y]
        second = keep_out[1, y] + recv_out[1, y]
        msg[y, ROWS_IN : ROWS_IN + ROWS_OUT] = jnp.where(row <= col, first, second).astype(bf16)
        diag = jnp.sum(jnp.where(row == col, second, 0.0), axis=0, keepdims=True)
        top = lax.broadcasted_iota(jnp.int32, (ROWS_EXTRA, 128), 0) == 0
        msg[y, ROWS_IN + ROWS_OUT :] = jnp.where(top, diag, 0.0).astype(bf16)
        for zh in range(2):
            rows = (keep_in[zh, y] + recv_in[zh, y]).astype(bf16)
            for c in range(8):
                msg[y, c * 32 + zh * 16 : c * 32 + zh * 16 + 16] = rows[:, c * 128 : c * 128 + 128]


def pack(keep_out, recv_out, keep_in, recv_in):
    outs = pl.BlockSpec((2, 4, 128, 128), lambda x: (x, 0, 0, 0))
    ins = pl.BlockSpec((2, 4, 16, 1024), lambda x: (x, 0, 0, 0))
    return pl.pallas_call(
        pack_kernel,
        grid=(4,),
        in_specs=[outs, outs, ins, ins],
        out_specs=pl.BlockSpec((4, ROWS, 128), lambda x: (x, 0, 0)),
        out_shape=jax.ShapeDtypeStruct((16, ROWS, 128), bf16),
        compiler_params=pltpu.CompilerParams(vmem_limit_bytes=VMEM),
        cost_estimate=pl.CostEstimate(flops=4 << 20, bytes_accessed=10 << 20, transcendentals=0),
        name="pack",
    )(
        keep_out.reshape(8, 4, 128, 128),
        recv_out.reshape(8, 4, 128, 128),
        keep_in.reshape(8, 4, 16, 1024),
        recv_in.reshape(8, 4, 16, 1024),
    )


def precond_kernel(meta, q_own, q_other, grad, q_out, values_in, values_out, precond, parts, full):
    core, zh = meta[0], meta[3]
    for x in range(4):
        for y in range(4):
            for p in range(2):
                z = zh if p == 0 else 1 - zh
                slab = ((x * 2 + z) * 4 + y) * 2
                for src, c in ((q_own, core), (q_other, 1 - core)):
                    at = pl.multiple_of((slab + c) * 16, 16)
                    full[pl.ds(at, 16), :] = src[x * 4 + y, p * 16 : p * 16 + 16, :]
    basis = full[...]
    g = grad[...]
    q = q_out[...]
    rotated = dot(g, basis, 0, 0).astype(bf16)
    spectral = dot(q, rotated, 0, 0)
    scaled = (spectral / (values_in[...] * values_out[...] + damping)).astype(bf16)
    back_rot = dot(q, scaled, 1, 0).astype(bf16)
    result = dot(basis, back_rot, 1, 1)
    precond[...] = result
    inner = jnp.sum(jnp.sum(result * g.astype(f32), axis=0, keepdims=True), axis=1, keepdims=True)
    high = inner.astype(bf16).astype(f32)
    rest = inner - high
    middle = rest.astype(bf16).astype(f32)
    low = rest - middle
    row = lax.broadcasted_iota(jnp.int32, (16, 128), 0)
    parts[...] = jnp.where(
        row == 1, high, jnp.where(row == 2, middle, jnp.where(row == 3, low, 0.0))
    ).astype(bf16)


def precondition(meta, q_own, q_other, grad, q_out, values_in, values_out):
    whole = pl.BlockSpec(memory_space=pltpu.VMEM)
    return pl.pallas_call(
        precond_kernel,
        in_specs=[pl.BlockSpec(memory_space=pltpu.SMEM)] + [whole] * 6,
        out_specs=[whole, whole],
        out_shape=[jax.ShapeDtypeStruct((1024, 128), f32), jax.ShapeDtypeStruct((16, 128), bf16)],
        scratch_shapes=[pltpu.VMEM((1024, 1024), bf16)],
        compiler_params=pltpu.CompilerParams(vmem_limit_bytes=VMEM),
        cost_estimate=pl.CostEstimate(flops=600 << 20, bytes_accessed=3 << 20, transcendentals=0),
        name="precondition",
    )(meta, q_own, q_other, grad, q_out, values_in, values_out)


def unpack_kernel(meta, msg, column, keep_in, send_in):
    first = meta[3] == 0

    def total(at, rows):
        out = msg[0, at : at + rows].astype(f32)
        for s in range(1, 16):
            out = out + msg[s, at : at + rows].astype(f32)
        return out

    for c in range(8):
        pair = total(c * 32, 32)
        lo, hi = pair[:16], pair[16:]
        keep_in[:, c * 128 : c * 128 + 128] = jnp.where(first, lo, hi)
        send_in[:, c * 128 : c * 128 + 128] = jnp.where(first, hi, lo)
    folded = total(ROWS_IN, ROWS_OUT)
    extra = total(ROWS_IN + ROWS_OUT, ROWS_EXTRA)
    turned = folded.T
    row = lax.broadcasted_iota(jnp.int32, (128, 128), 0)
    col = lax.broadcasted_iota(jnp.int32, (128, 128), 1)
    one = jnp.where(row <= col, folded, turned)
    two = jnp.where(row > col, folded, jnp.where(row == col, extra[0:1], turned))
    inner = jnp.broadcast_to(extra[1:2] + extra[2:3] + extra[3:4], (8, 128))
    for z in range(4):
        column[z, 0:32] = one[z * 32 : z * 32 + 32]
        column[4 + z, 0:32] = two[z * 32 : z * 32 + 32]
        column[z, 32:40] = inner
        column[4 + z, 32:40] = inner


def unpack(meta, msg):
    whole = pl.BlockSpec(memory_space=pltpu.VMEM)
    return pl.pallas_call(
        unpack_kernel,
        in_specs=[pl.BlockSpec(memory_space=pltpu.SMEM), whole],
        out_specs=[whole] * 3,
        out_shape=[
            jax.ShapeDtypeStruct((8, 40, 128), f32),
            jax.ShapeDtypeStruct((16, 1024), f32),
            jax.ShapeDtypeStruct((16, 1024), f32),
        ],
        compiler_params=pltpu.CompilerParams(vmem_limit_bytes=VMEM),
        cost_estimate=pl.CostEstimate(flops=2 << 20, bytes_accessed=2 << 20, transcendentals=0),
        name="unpack",
    )(meta, msg)


def swap(array, axis):
    return lax.ppermute(array, axis, [(0, 1), (1, 0)])


def local(
    activations,
    output_grads,
    token_counts,
    owner_blocks,
    basis_in,
    basis_out,
    values_in,
    values_out,
    gradient,
    learning_rate,
):
    core = lax.axis_index("core").astype(jnp.int32)
    zh = lax.axis_index("zh").astype(jnp.int32)
    zl = lax.axis_index("zl").astype(jnp.int32)
    own_count = lax.dynamic_slice_in_dim(token_counts, lax.axis_index(DP), 1)[0]
    token_total = jnp.sum(token_counts).astype(f32)
    quarter = output_grads.shape[0]
    meta = jnp.stack([core, own_count - zl * quarter, own_count, zh])

    mine = basis_in[0]
    slabs = jnp.concatenate([mine, swap(mine, "zh")], axis=0)

    send_out, keep_out = cov_out_partial(output_grads, owner_blocks, meta)
    recv_out = swap(send_out, "core")
    send_in, keep_in = cov_in_partial(activations, meta)
    recv_in = swap(send_in, "core")

    q_own = lax.all_to_all(
        jnp.broadcast_to(slabs[None], (16,) + slabs.shape), PLANE, 0, 0, tiled=True
    )
    q_other = swap(q_own, "core")
    msg = pack(keep_out, recv_out, keep_in, recv_in)
    precond, parts = precondition(
        meta, q_own, q_other, gradient, basis_out[0], values_in[None, :], values_out[:, None]
    )
    at = ROWS_IN + ROWS_OUT + 1
    msg = lax.dynamic_update_slice(
        msg, jnp.broadcast_to(parts[None, 1:4], (16, 3, 128)), (0, at, 0)
    )
    msg = lax.all_to_all(msg, PLANE, 0, 0, tiled=True)
    column, keep_slab, send_slab = unpack(meta, msg)
    recv_slab = swap(send_slab, "zh")
    column = lax.all_to_all(column, COLUMN, 0, 0, tiled=True)
    cov_in = ((keep_slab + recv_slab) / token_total)[None]
    cov_out = (jnp.sum(column[:, :32], axis=0) / token_total)[None]
    inner = jnp.sum(column[:, 32, :1], axis=0)
    inner = (inner + swap(inner, "core"))[0]
    clip_factor = jnp.minimum(
        1.0, jnp.sqrt(kl_clip / (learning_rate[0] * learning_rate[0] * inner))
    )
    update = clip_factor * precond
    return (cov_in, cov_out, update)


def solution(mesh):
    fine = Mesh(mesh.devices.reshape(SIZES), AXES)
    placed = (
        P(DP, "zl"),
        P(AXES, None),
        P(),
        P(),
        P("zl", DP, None),
        P(DP, None, None),
        P("zl"),
        P(DP),
        P("zl", DP),
        P(),
    )
    return jax.shard_map(
        local,
        mesh=fine,
        in_specs=placed,
        out_specs=(P("zl", DP, None), P(DP, "zl", None), P("zl", DP)),
        check_vma=False,
    )
```

```python
import jax
import jax.numpy as jnp
from jax import lax
from jax.experimental import pallas as pl
from jax.experimental.pallas import tpu as pltpu
from jax.sharding import Mesh, PartitionSpec as P

damping = 0.03
kl_clip = 0.001
f32 = jnp.float32
bf16 = jnp.bfloat16

AXES = ("x", "zh", "y", "core", "zl")
SIZES = (4, 2, 4, 2, 4)
DP = ("x", "zh", "y", "core")
PLANE = ("x", "y")
COLUMN = ("zh", "zl")
VMEM = 20 << 20

ROWS_IN = 256
ROWS_OUT = 128
ROWS_EXTRA = 16
ROWS = ROWS_IN + ROWS_OUT + ROWS_EXTRA


def dot(a, b, ca, cb):
    return lax.dot_general(a, b, (((ca,), (cb,)), ((), ())), preferred_element_type=f32)


def counted():
    core = lax.axis_index("core")
    dp = ((lax.axis_index("x") * 2 + lax.axis_index("zh")) * 4 + lax.axis_index("y")) * 2 + core
    return dp, core, lax.axis_index("zl")


def cov_out_kernel(owners, counts, core, *refs):
    blocks, (send, keep) = refs[:8], refs[8:]
    dp, _, zl = counted()
    quarter = blocks[0].shape[0]
    live = counts[dp] - zl * quarter
    rows = lax.broadcasted_iota(jnp.int32, blocks[0].shape, 0) < live
    for y in range(4):
        for src, dst in ((blocks[y], keep), (blocks[4 + y], send)):
            full = src[...]
            masked = jnp.where(rows, full, jnp.zeros((), bf16))
            dst[y] = dot(masked, full, 0, 0)


def cov_out_partial(output_grads, owners, counts, core):
    quarter = output_grads.shape[0]

    def at(y, other):
        def index(s, owners, counts, core):
            c = 1 - core[0] if other else core[0]
            return (0, owners[(s * 4 + y) * 2 + c])

        return pl.BlockSpec((quarter, 128), index)

    out = pl.BlockSpec((4, 128, 128), lambda s, *_: (s, 0, 0))
    return pl.pallas_call(
        cov_out_kernel,
        grid_spec=pltpu.PrefetchScalarGridSpec(
            num_scalar_prefetch=3,
            grid=(8,),
            in_specs=[at(y, False) for y in range(4)] + [at(y, True) for y in range(4)],
            out_specs=[out, out],
        ),
        out_shape=[jax.ShapeDtypeStruct((32, 128, 128), f32)] * 2,
        compiler_params=pltpu.CompilerParams(vmem_limit_bytes=VMEM),
        cost_estimate=pl.CostEstimate(
            flops=2 * quarter * 8192 * 128, bytes_accessed=quarter * 8192 * 2 + (4 << 20), transcendentals=0
        ),
        name="cov_out_partial",
    )(owners, counts, core, *([output_grads] * 8))


def cov_in_kernel(counts, lhs, rhs, send, keep):
    dp, core, _ = counted()
    first = core == 0
    rows = lax.broadcasted_iota(jnp.int32, lhs.shape, 0) < counts[dp]
    masked = jnp.where(rows, lhs[...], jnp.zeros((), bf16))
    part = dot(masked, rhs[...], 0, 0).reshape(8, 2, 16, 1024)
    keep[...] = jnp.where(first, part[:, 0], part[:, 1])
    send[...] = jnp.where(first, part[:, 1], part[:, 0])


def cov_in_partial(activations, counts):
    tok = activations.shape[0]
    out = pl.BlockSpec((8, 16, 1024), lambda s, *_: (s, 0, 0))
    return pl.pallas_call(
        cov_in_kernel,
        grid_spec=pltpu.PrefetchScalarGridSpec(
            num_scalar_prefetch=1,
            grid=(4,),
            in_specs=[
                pl.BlockSpec((tok, 256), lambda s, *_: (0, s)),
                pl.BlockSpec((tok, 1024), lambda s, *_: (0, 0)),
            ],
            out_specs=[out, out],
        ),
        out_shape=[jax.ShapeDtypeStruct((32, 16, 1024), f32)] * 2,
        compiler_params=pltpu.CompilerParams(vmem_limit_bytes=VMEM),
        cost_estimate=pl.CostEstimate(
            flops=2 * tok * 1024 * 1024, bytes_accessed=tok * 4096 + (4 << 20), transcendentals=0
        ),
        name="cov_in_partial",
    )(counts, activations, activations)


def pack_kernel(keep_out, recv_out, keep_in, recv_in, msg):
    row = lax.broadcasted_iota(jnp.int32, (128, 128), 0)
    col = lax.broadcasted_iota(jnp.int32, (128, 128), 1)
    for y in range(4):
        first = keep_out[0, y] + recv_out[0, y]
        second = keep_out[1, y] + recv_out[1, y]
        msg[y, ROWS_IN : ROWS_IN + ROWS_OUT] = jnp.where(row <= col, first, second).astype(bf16)
        diag = jnp.sum(jnp.where(row == col, second, 0.0), axis=0, keepdims=True)
        top = lax.broadcasted_iota(jnp.int32, (ROWS_EXTRA, 128), 0) == 0
        msg[y, ROWS_IN + ROWS_OUT :] = jnp.where(top, diag, 0.0).astype(bf16)
        for zh in range(2):
            rows = (keep_in[zh, y] + recv_in[zh, y]).astype(bf16)
            for c in range(8):
                msg[y, c * 32 + zh * 16 : c * 32 + zh * 16 + 16] = rows[:, c * 128 : c * 128 + 128]


def pack(keep_out, recv_out, keep_in, recv_in):
    outs = pl.BlockSpec((2, 4, 128, 128), lambda x: (x, 0, 0, 0))
    ins = pl.BlockSpec((2, 4, 16, 1024), lambda x: (x, 0, 0, 0))
    return pl.pallas_call(
        pack_kernel,
        grid=(4,),
        in_specs=[outs, outs, ins, ins],
        out_specs=pl.BlockSpec((4, ROWS, 128), lambda x: (x, 0, 0)),
        out_shape=jax.ShapeDtypeStruct((16, ROWS, 128), bf16),
        compiler_params=pltpu.CompilerParams(vmem_limit_bytes=VMEM),
        cost_estimate=pl.CostEstimate(flops=4 << 20, bytes_accessed=10 << 20, transcendentals=0),
        name="pack",
    )(
        keep_out.reshape(8, 4, 128, 128),
        recv_out.reshape(8, 4, 128, 128),
        keep_in.reshape(8, 4, 16, 1024),
        recv_in.reshape(8, 4, 16, 1024),
    )


def dot_slabs(left, slabs, core):
    picked = jnp.concatenate(
        [left[pl.ds(pl.multiple_of((2 * s + core) * 16, 16), 16), :] for s in range(32)], axis=0
    )
    return dot(picked, slabs[...].reshape(512, 1024), 0, 0)


def rotate_kernel(slabs, grad, rotated):
    rotated[...] = dot_slabs(grad, slabs, lax.axis_index("core"))


def scale_kernel(slabs, grad, partial, q_out, values_in, values_out, back, parts):
    total = partial[...] + dot_slabs(grad, slabs, 1 - lax.axis_index("core"))
    q = q_out[...]
    spectral = dot(q, total.astype(bf16), 0, 0)
    scaled = (spectral / (values_in[...] * values_out[...] + damping)).astype(bf16)
    back_rot = dot(q, scaled, 1, 0).astype(bf16)
    back[...] = back_rot
    inner = jnp.sum(
        jnp.sum(back_rot.astype(f32) * total, axis=0, keepdims=True), axis=1, keepdims=True
    )
    high = inner.astype(bf16).astype(f32)
    rest = inner - high
    middle = rest.astype(bf16).astype(f32)
    low = rest - middle
    row = lax.broadcasted_iota(jnp.int32, (16, 128), 0)
    parts[...] = jnp.where(
        row == 1, high, jnp.where(row == 2, middle, jnp.where(row == 3, low, 0.0))
    ).astype(bf16)


def finish_kernel(q_own, q_other, back, precond):
    core = lax.axis_index("core")
    for src, c in ((q_own, core), (q_other, 1 - core)):
        result = dot(src[...].reshape(512, 1024), back[...], 1, 1)
        for s in range(32):
            at = pl.multiple_of((2 * s + c) * 16, 16)
            precond[pl.ds(at, 16), :] = result[s * 16 : s * 16 + 16]


def on_chip(kernel, outs, flops, *args):
    whole = pl.BlockSpec(memory_space=pltpu.VMEM)
    size = sum(a.size * a.dtype.itemsize for a in args)
    return pl.pallas_call(
        kernel,
        in_specs=[whole] * len(args),
        out_specs=[whole] * len(outs),
        out_shape=outs,
        compiler_params=pltpu.CompilerParams(vmem_limit_bytes=VMEM),
        cost_estimate=pl.CostEstimate(flops=flops, bytes_accessed=size, transcendentals=0),
        name=kernel.__name__[:-7],
    )(*args)


def unpack_kernel(msg, column, keep_in, send_in):
    first = lax.axis_index("zh") == 0

    def total(at, rows):
        out = msg[0, at : at + rows].astype(f32)
        for s in range(1, 16):
            out = out + msg[s, at : at + rows].astype(f32)
        return out

    for c in range(8):
        pair = total(c * 32, 32)
        lo, hi = pair[:16], pair[16:]
        keep_in[:, c * 128 : c * 128 + 128] = jnp.where(first, lo, hi)
        send_in[:, c * 128 : c * 128 + 128] = jnp.where(first, hi, lo)
    folded = total(ROWS_IN, ROWS_OUT)
    extra = total(ROWS_IN + ROWS_OUT, ROWS_EXTRA)
    turned = folded.T
    row = lax.broadcasted_iota(jnp.int32, (128, 128), 0)
    col = lax.broadcasted_iota(jnp.int32, (128, 128), 1)
    one = jnp.where(row <= col, folded, turned)
    two = jnp.where(row > col, folded, jnp.where(row == col, extra[0:1], turned))
    row = lax.broadcasted_iota(jnp.int32, extra.shape, 0)
    inner = jnp.sum(jnp.where((row >= 1) & (row < 7), extra, 0.0), axis=0, keepdims=True)
    inner = jnp.broadcast_to(inner, (8, 128))
    for z in range(4):
        column[z, 0:32] = one[z * 32 : z * 32 + 32]
        column[4 + z, 0:32] = two[z * 32 : z * 32 + 32]
        column[z, 32:40] = inner
        column[4 + z, 32:40] = inner


def swap(array, axis):
    return lax.ppermute(array, axis, [(0, 1), (1, 0)])


def local(
    activations,
    output_grads,
    token_counts,
    owner_blocks,
    basis_in,
    basis_out,
    values_in,
    values_out,
    gradient,
    learning_rate,
):
    token_total = jnp.sum(token_counts).astype(f32)
    shape = jax.ShapeDtypeStruct
    slabs = jnp.broadcast_to(basis_in, (32,) + basis_in.shape[1:])
    q_own = lax.all_to_all(slabs, ("x", "zh", "y"), 0, 0, tiled=True)

    core = lax.axis_index("core").astype(jnp.int32)[None]
    send_out, keep_out = cov_out_partial(output_grads, owner_blocks, token_counts, core)
    recv_out = swap(send_out, "core")
    send_in, keep_in = cov_in_partial(activations, token_counts)
    recv_in = swap(send_in, "core")
    msg = pack(keep_out, recv_out, keep_in, recv_in)

    q_other = swap(q_own, "core")
    (partial,) = on_chip(rotate_kernel, [shape((128, 1024), f32)], 128 << 20, q_own, gradient)
    back, parts = on_chip(
        scale_kernel,
        [shape((128, 1024), bf16), shape((16, 128), bf16)],
        256 << 20,
        q_other,
        gradient,
        partial,
        basis_out[0],
        values_in[None, :],
        values_out[:, None],
    )
    parts = jnp.concatenate([parts[1:4], swap(parts, "core")[1:4]], axis=0)
    (precond,) = on_chip(finish_kernel, [shape((1024, 128), f32)], 256 << 20, q_own, q_other, back)
    at = ROWS_IN + ROWS_OUT + 1
    msg = lax.dynamic_update_slice(
        msg, jnp.broadcast_to(parts[None], (16, 6, 128)), (0, at, 0)
    )
    msg = lax.all_to_all(msg, PLANE, 0, 0, tiled=True)
    column, keep_slab, send_slab = on_chip(
        unpack_kernel,
        [shape((8, 40, 128), f32), shape((16, 1024), f32), shape((16, 1024), f32)],
        2 << 20,
        msg,
    )
    recv_slab = swap(send_slab, "zh")
    column = lax.all_to_all(column, COLUMN, 0, 0, tiled=True)
    cov_in = ((keep_slab + recv_slab) / token_total)[None]
    cov_out = (jnp.sum(column[:, :32], axis=0) / token_total)[None]
    inner = jnp.sum(column[:, 32, 0], axis=0)
    clip_factor = jnp.minimum(
        1.0, jnp.sqrt(kl_clip / (learning_rate[0] * learning_rate[0] * inner))
    )
    update = clip_factor * precond
    return (cov_in, cov_out, update)


def solution(mesh):
    fine = Mesh(mesh.devices.reshape(SIZES), AXES)
    placed = (
        P(DP, "zl"),
        P(AXES, None),
        P(),
        P(),
        P("zl", DP, None),
        P(DP, None, None),
        P("zl"),
        P(DP),
        P("zl", DP),
        P(),
    )
    return jax.shard_map(
        local,
        mesh=fine,
        in_specs=placed,
        out_specs=(P("zl", DP, None), P(DP, "zl", None), P("zl", DP)),
        check_vma=False,
    )
```

```python
import jax
import jax.numpy as jnp
from jax import lax
from jax.experimental import pallas as pl
from jax.experimental.pallas import tpu as pltpu
from jax.sharding import Mesh, PartitionSpec as P

damping = 0.03
kl_clip = 0.001
f32 = jnp.float32
bf16 = jnp.bfloat16

AXES = ("x", "zh", "y", "core", "zl")
SIZES = (4, 2, 4, 2, 4)
DP = ("x", "zh", "y", "core")
PLANE = ("x", "y")
COLUMN = ("zh", "zl")
VMEM = 20 << 20

ROWS_IN = 256
ROWS_OUT = 128
ROWS_EXTRA = 16
ROWS = ROWS_IN + ROWS_OUT + ROWS_EXTRA


def dot(a, b, ca, cb):
    return lax.dot_general(a, b, (((ca,), (cb,)), ((), ())), preferred_element_type=f32)


def counted():
    core = lax.axis_index("core")
    dp = ((lax.axis_index("x") * 2 + lax.axis_index("zh")) * 4 + lax.axis_index("y")) * 2 + core
    return dp, core, lax.axis_index("zl")


def cov_out_kernel(owners, counts, core, *refs):
    blocks, (send, keep) = refs[:8], refs[8:]
    dp, _, zl = counted()
    quarter = blocks[0].shape[0]
    live = counts[dp] - zl * quarter
    rows = lax.broadcasted_iota(jnp.int32, blocks[0].shape, 0) < live
    row = lax.broadcasted_iota(jnp.int32, (128, 128), 0)
    col = lax.broadcasted_iota(jnp.int32, (128, 128), 1)
    top = lax.broadcasted_iota(jnp.int32, (ROWS_EXTRA, 128), 0) == 0

    def product(ref):
        full = ref[...]
        return dot(jnp.where(rows, full, jnp.zeros((), bf16)), full, 0, 0)

    for y in range(2):
        for at, dst in ((0, keep), (4, send)):
            first = product(blocks[at + y])
            second = product(blocks[at + 2 + y])
            diag = jnp.sum(jnp.where(row == col, second, 0.0), axis=0, keepdims=True)
            dst[y, 0:ROWS_OUT] = jnp.where(row <= col, first, second).astype(dst.dtype)
            dst[y, ROWS_OUT:] = jnp.where(top, diag, 0.0).astype(dst.dtype)


def cov_out_partial(output_grads, owners, counts, core):
    quarter = output_grads.shape[0]

    def at(zh, y, other):
        def index(s, owners, counts, core):
            c = 1 - core[0] if other else core[0]
            x, half = s // 2, s % 2
            return (0, owners[((x * 2 + zh) * 4 + half * 2 + y) * 2 + c])

        return pl.BlockSpec((quarter, 128), index)

    rows = ROWS_OUT + ROWS_EXTRA
    out = pl.BlockSpec((2, rows, 128), lambda s, *_: (s, 0, 0))
    order = [(zh, y, other) for other in (False, True) for zh in range(2) for y in range(2)]
    return pl.pallas_call(
        cov_out_kernel,
        grid_spec=pltpu.PrefetchScalarGridSpec(
            num_scalar_prefetch=3,
            grid=(8,),
            in_specs=[at(*o) for o in order],
            out_specs=[out, out],
        ),
        out_shape=[
            jax.ShapeDtypeStruct((16, rows, 128), bf16),
            jax.ShapeDtypeStruct((16, rows, 128), f32),
        ],
        compiler_params=pltpu.CompilerParams(vmem_limit_bytes=60 << 20),
        cost_estimate=pl.CostEstimate(
            flops=2 * quarter * 8192 * 128, bytes_accessed=quarter * 8192 * 2 + (4 << 20), transcendentals=0
        ),
        name="cov_out_partial",
    )(owners, counts, core, *([output_grads] * 8))


def cov_in_kernel(counts, lhs, rhs, send, keep):
    dp, core, _ = counted()
    first = core == 0
    rows = lax.broadcasted_iota(jnp.int32, lhs.shape, 0) < counts[dp]
    masked = jnp.where(rows, lhs[...], jnp.zeros((), bf16))
    part = dot(masked, rhs[...], 0, 0)
    for zh in range(2):
        for y in range(4):
            at = (zh * 4 + y) * 32
            low, high = part[at : at + 16], part[at + 16 : at + 32]
            for dst, rows in (
                (keep, jnp.where(first, low, high)),
                (send, jnp.where(first, high, low).astype(bf16)),
            ):
                for c in range(8):
                    at = c * 32 + zh * 16
                    dst[y, at : at + 16] = rows[:, c * 128 : c * 128 + 128]


def cov_in_partial(activations, counts):
    tok = activations.shape[0]
    out = pl.BlockSpec((4, ROWS_IN, 128), lambda s, *_: (s, 0, 0))
    return pl.pallas_call(
        cov_in_kernel,
        grid_spec=pltpu.PrefetchScalarGridSpec(
            num_scalar_prefetch=1,
            grid=(4,),
            in_specs=[
                pl.BlockSpec((tok, 256), lambda s, *_: (0, s)),
                pl.BlockSpec((tok, 1024), lambda s, *_: (0, 0)),
            ],
            out_specs=[out, out],
        ),
        out_shape=[
            jax.ShapeDtypeStruct((16, ROWS_IN, 128), bf16),
            jax.ShapeDtypeStruct((16, ROWS_IN, 128), f32),
        ],
        compiler_params=pltpu.CompilerParams(vmem_limit_bytes=VMEM),
        cost_estimate=pl.CostEstimate(
            flops=2 * tok * 1024 * 1024, bytes_accessed=tok * 4096 + (4 << 20), transcendentals=0
        ),
        name="cov_in_partial",
    )(counts, activations, activations)


def pack_kernel(keep_in, recv_in, keep_out, recv_out, msg):
    def step(s, _):
        msg[s, 0:ROWS_IN] = (keep_in[s] + recv_in[s].astype(f32)).astype(bf16)
        msg[s, ROWS_IN:] = (keep_out[s] + recv_out[s].astype(f32)).astype(bf16)
        return 0

    lax.fori_loop(0, 16, step, 0)


def slab_rows(core):
    zh = lax.axis_index("zh")
    for x in range(4):
        for y in range(4):
            for z in (zh, 1 - zh):
                slab = ((x * 2 + z) * 4 + y) * 2 + core
                yield pl.ds(pl.multiple_of(slab * 16, 16), 16)


def dot_slabs(left, slabs, core):
    picked = jnp.concatenate([left[rows, :] for rows in slab_rows(core)], axis=0)
    return dot(picked, slabs[...].reshape(512, 1024), 0, 0)


def rotate_kernel(slabs, grad, rotated):
    rotated[...] = dot_slabs(grad, slabs, lax.axis_index("core"))


def scale_kernel(slabs, grad, partial, q_out, values_in, values_out, back, parts):
    total = partial[...] + dot_slabs(grad, slabs, 1 - lax.axis_index("core"))
    q = q_out[...]
    spectral = dot(q, total.astype(bf16), 0, 0)
    scaled = (spectral / (values_in[...] * values_out[...] + damping)).astype(bf16)
    back_rot = dot(q, scaled, 1, 0).astype(bf16)
    back[...] = back_rot
    inner = jnp.sum(
        jnp.sum(back_rot.astype(f32) * total, axis=0, keepdims=True), axis=1, keepdims=True
    )
    high = inner.astype(bf16).astype(f32)
    rest = inner - high
    middle = rest.astype(bf16).astype(f32)
    low = rest - middle
    row = lax.broadcasted_iota(jnp.int32, (16, 128), 0)
    parts[...] = jnp.where(
        row == 1, high, jnp.where(row == 2, middle, jnp.where(row == 3, low, 0.0))
    ).astype(bf16)


def finish_kernel(q_own, q_other, back, precond):
    core = lax.axis_index("core")
    for src, c in ((q_own, core), (q_other, 1 - core)):
        result = dot(src[...].reshape(512, 1024), back[...], 1, 1)
        for s, rows in enumerate(slab_rows(c)):
            precond[rows, :] = result[s * 16 : s * 16 + 16]


def clip_kernel(scalars, column, precond, cov_out, update):
    total = jnp.sum(column[...], axis=0)
    cov_out[0] = total[0:32] / scalars[0]
    rate = scalars[1]
    update[...] = jnp.minimum(1.0, jnp.sqrt(kl_clip / (rate * rate * total[32:33]))) * precond[...]


def on_chip(kernel, outs, flops, *args):
    whole = pl.BlockSpec(memory_space=pltpu.VMEM)
    size = sum(a.size * a.dtype.itemsize for a in args)
    return pl.pallas_call(
        kernel,
        in_specs=[whole if a.ndim > 1 else pl.BlockSpec(memory_space=pltpu.SMEM) for a in args],
        out_specs=[whole] * len(outs),
        out_shape=outs,
        compiler_params=pltpu.CompilerParams(vmem_limit_bytes=VMEM),
        cost_estimate=pl.CostEstimate(flops=flops, bytes_accessed=size, transcendentals=0),
        name=kernel.__name__[:-7],
    )(*args)


def unpack_kernel(msg, column, keep_in, send_in):
    first = lax.axis_index("zh") == 0

    def total(at, rows):
        out = msg[0, at : at + rows].astype(f32)
        for s in range(1, 16):
            out = out + msg[s, at : at + rows].astype(f32)
        return out

    for c in range(8):
        pair = total(c * 32, 32)
        lo, hi = pair[:16], pair[16:]
        keep_in[:, c * 128 : c * 128 + 128] = jnp.where(first, lo, hi)
        send_in[:, c * 128 : c * 128 + 128] = jnp.where(first, hi, lo)
    folded = total(ROWS_IN, ROWS_OUT)
    extra = total(ROWS_IN + ROWS_OUT, ROWS_EXTRA)
    turned = folded.T
    row = lax.broadcasted_iota(jnp.int32, (128, 128), 0)
    col = lax.broadcasted_iota(jnp.int32, (128, 128), 1)
    one = jnp.where(row <= col, folded, turned)
    two = jnp.where(row > col, folded, jnp.where(row == col, extra[0:1], turned))
    row = lax.broadcasted_iota(jnp.int32, extra.shape, 0)
    inner = jnp.sum(jnp.where((row >= 1) & (row < 7), extra, 0.0), axis=0, keepdims=True)
    inner = jnp.broadcast_to(inner, (8, 128))
    for z in range(4):
        column[z, 0:32] = one[z * 32 : z * 32 + 32]
        column[4 + z, 0:32] = two[z * 32 : z * 32 + 32]
        column[z, 32:40] = inner
        column[4 + z, 32:40] = inner


def swap(array, axis):
    return lax.ppermute(array, axis, [(0, 1), (1, 0)])


def local(
    activations,
    output_grads,
    token_counts,
    owner_blocks,
    basis_in,
    basis_out,
    values_in,
    values_out,
    gradient,
    learning_rate,
):
    token_total = jnp.sum(token_counts).astype(f32)
    shape = jax.ShapeDtypeStruct
    core = lax.axis_index("core").astype(jnp.int32)[None]
    mine = basis_in[0]
    slabs = jnp.concatenate([mine, swap(mine, "zh")], axis=0)
    send_out, keep_out = cov_out_partial(output_grads, owner_blocks, token_counts, core)
    slabs, send_out, counts = lax.optimization_barrier((slabs, send_out, token_counts))
    q_own = lax.all_to_all(
        jnp.broadcast_to(slabs[None], (16,) + slabs.shape), PLANE, 0, 0, tiled=True
    )
    recv_out = swap(send_out, "core")
    send_in, keep_in = cov_in_partial(activations, counts)
    recv_in = swap(send_in, "core")
    q_own, keep_in, recv_out = lax.optimization_barrier((q_own, keep_in, recv_out))
    (msg,) = on_chip(
        pack_kernel, [shape((16, ROWS, 128), bf16)], 1 << 20, keep_in, recv_in, keep_out, recv_out
    )

    q_other = swap(q_own, "core")
    (partial,) = on_chip(rotate_kernel, [shape((128, 1024), f32)], 128 << 20, q_own, gradient)
    back, parts = on_chip(
        scale_kernel,
        [shape((128, 1024), bf16), shape((16, 128), bf16)],
        256 << 20,
        q_other,
        gradient,
        partial,
        basis_out[0],
        values_in[None, :],
        values_out[:, None],
    )
    other_parts, msg = lax.optimization_barrier((swap(parts, "core"), msg))
    parts = jnp.concatenate([parts[1:4], other_parts[1:4]], axis=0)
    (precond,) = on_chip(finish_kernel, [shape((1024, 128), f32)], 256 << 20, q_own, q_other, back)
    at = ROWS_IN + ROWS_OUT + 1
    msg = lax.dynamic_update_slice(
        msg, jnp.broadcast_to(parts[None], (16, 6, 128)), (0, at, 0)
    )
    msg = lax.all_to_all(msg, PLANE, 0, 0, tiled=True)
    column, keep_slab, send_slab = on_chip(
        unpack_kernel,
        [shape((8, 40, 128), f32), shape((16, 1024), f32), shape((16, 1024), f32)],
        2 << 20,
        msg,
    )
    recv_slab = swap(send_slab, "zh")
    column = lax.all_to_all(column, COLUMN, 0, 0, tiled=True)
    cov_in = ((keep_slab + recv_slab) / token_total)[None]
    cov_out, update = on_chip(
        clip_kernel,
        [shape((1, 32, 128), f32), shape((1024, 128), f32)],
        1 << 20,
        jnp.stack([token_total, learning_rate[0]]),
        column,
        precond,
    )
    return (cov_in, cov_out, update)


def solution(mesh):
    fine = Mesh(mesh.devices.reshape(SIZES), AXES)
    placed = (
        P(DP, "zl"),
        P(AXES, None),
        P(),
        P(),
        P("zl", DP, None),
        P(DP, None, None),
        P("zl"),
        P(DP),
        P("zl", DP),
        P(),
    )
    return jax.shard_map(
        local,
        mesh=fine,
        in_specs=placed,
        out_specs=(P("zl", DP, None), P(DP, "zl", None), P("zl", DP)),
        check_vma=False,
    )
```

```python
import jax
import jax.numpy as jnp
from jax import lax
from jax.experimental import pallas as pl
from jax.experimental.pallas import tpu as pltpu
from jax.sharding import Mesh, PartitionSpec as P

damping = 0.03
kl_clip = 0.001
f32 = jnp.float32
bf16 = jnp.bfloat16

AXES = ("x", "zh", "y", "core", "zl")
SIZES = (4, 2, 4, 2, 4)
DP = ("x", "zh", "y", "core")
PLANE = ("x", "y")
COLUMN = ("zh", "zl")
VMEM = 20 << 20

ROWS_IN = 256
ROWS_OUT = 128
ROWS_EXTRA = 16


def dot(a, b, ca, cb):
    return lax.dot_general(a, b, (((ca,), (cb,)), ((), ())), preferred_element_type=f32)


def counted():
    core = lax.axis_index("core")
    dp = ((lax.axis_index("x") * 2 + lax.axis_index("zh")) * 4 + lax.axis_index("y")) * 2 + core
    return dp, core, lax.axis_index("zl")


def cov_out_kernel(owners, counts, core, *refs):
    blocks, (send, keep) = refs[:8], refs[8:]
    dp, _, zl = counted()
    quarter = blocks[0].shape[0]
    live = counts[dp] - zl * quarter
    rows = lax.broadcasted_iota(jnp.int32, blocks[0].shape, 0) < live
    row = lax.broadcasted_iota(jnp.int32, (128, 128), 0)
    col = lax.broadcasted_iota(jnp.int32, (128, 128), 1)
    top = lax.broadcasted_iota(jnp.int32, (ROWS_EXTRA, 128), 0) == 0

    rows = jnp.concatenate([rows, rows], axis=1)
    for y in range(2):
        for at, dst in ((0, keep), (4, send)):
            full = jnp.concatenate([blocks[at + y][...], blocks[at + 2 + y][...]], axis=1)
            both = dot(jnp.where(rows, full, jnp.zeros((), bf16)), full, 0, 0)
            first, second = both[:128, :128], both[128:, 128:]
            diag = jnp.sum(jnp.where(row == col, second, 0.0), axis=0, keepdims=True)
            dst[y, 0:ROWS_OUT] = jnp.where(row <= col, first, second).astype(dst.dtype)
            dst[y, ROWS_OUT:] = jnp.where(top, diag, 0.0).astype(dst.dtype)


def cov_out_partial(output_grads, owners, counts, core):
    quarter = output_grads.shape[0]

    def at(zh, y, other):
        def index(s, owners, counts, core):
            c = 1 - core[0] if other else core[0]
            x, half = s // 2, s % 2
            return (0, owners[((x * 2 + zh) * 4 + half * 2 + y) * 2 + c])

        return pl.BlockSpec((quarter, 128), index)

    rows = ROWS_OUT + ROWS_EXTRA
    out = pl.BlockSpec((2, rows, 128), lambda s, *_: (s, 0, 0))
    order = [(zh, y, other) for other in (False, True) for zh in range(2) for y in range(2)]
    return pl.pallas_call(
        cov_out_kernel,
        grid_spec=pltpu.PrefetchScalarGridSpec(
            num_scalar_prefetch=3,
            grid=(8,),
            in_specs=[at(*o) for o in order],
            out_specs=[out, out],
        ),
        out_shape=[
            jax.ShapeDtypeStruct((16, rows, 128), bf16),
            jax.ShapeDtypeStruct((16, rows, 128), f32),
        ],
        compiler_params=pltpu.CompilerParams(vmem_limit_bytes=VMEM),
        cost_estimate=pl.CostEstimate(
            flops=2 * quarter * 8192 * 128, bytes_accessed=quarter * 8192 * 2 + (4 << 20), transcendentals=0
        ),
        name="cov_out_partial",
    )(owners, counts, core, *([output_grads] * 8))


def cov_in_kernel(counts, lhs, rhs, send, keep):
    dp, core, _ = counted()
    first = core == 0
    rows = lax.broadcasted_iota(jnp.int32, lhs.shape, 0) < counts[dp]
    masked = jnp.where(rows, lhs[...], jnp.zeros((), bf16))
    part = dot(masked, rhs[...], 0, 0)
    for zh in range(2):
        for y in range(4):
            at = (zh * 4 + y) * 32
            low, high = part[at : at + 16], part[at + 16 : at + 32]
            for dst, rows in (
                (keep, jnp.where(first, low, high)),
                (send, jnp.where(first, high, low).astype(bf16)),
            ):
                for c in range(8):
                    at = c * 32 + zh * 16
                    dst[y, at : at + 16] = rows[:, c * 128 : c * 128 + 128]


def cov_in_partial(activations, counts):
    tok = activations.shape[0]
    out = pl.BlockSpec((4, ROWS_IN, 128), lambda s, *_: (s, 0, 0))
    return pl.pallas_call(
        cov_in_kernel,
        grid_spec=pltpu.PrefetchScalarGridSpec(
            num_scalar_prefetch=1,
            grid=(4,),
            in_specs=[
                pl.BlockSpec((tok, 256), lambda s, *_: (0, s)),
                pl.BlockSpec((tok, 1024), lambda s, *_: (0, 0)),
            ],
            out_specs=[out, out],
        ),
        out_shape=[
            jax.ShapeDtypeStruct((16, ROWS_IN, 128), bf16),
            jax.ShapeDtypeStruct((16, ROWS_IN, 128), f32),
        ],
        compiler_params=pltpu.CompilerParams(vmem_limit_bytes=VMEM),
        cost_estimate=pl.CostEstimate(
            flops=2 * tok * 1024 * 1024, bytes_accessed=tok * 4096 + (4 << 20), transcendentals=0
        ),
        name="cov_in_partial",
    )(counts, activations, activations)


def pack_in_kernel(keep, recv, msg):
    def step(s, _):
        msg[s] = (keep[s] + recv[s].astype(f32)).astype(bf16)
        return 0

    lax.fori_loop(0, 16, step, 0)


def pack_out_kernel(keep, recv, inner, other_inner, msg):
    total = inner[0:1] + other_inner[0:1]
    high = total.astype(bf16).astype(f32)
    rest = total - high
    middle = rest.astype(bf16).astype(f32)
    low = rest - middle
    row = lax.broadcasted_iota(jnp.int32, (ROWS_EXTRA, 128), 0)
    parts = jnp.where(
        row == 1, high, jnp.where(row == 2, middle, jnp.where(row == 3, low, 0.0))
    )

    def step(s, _):
        both = keep[s] + recv[s].astype(f32)
        msg[s, 0:ROWS_OUT] = both[0:ROWS_OUT].astype(bf16)
        msg[s, ROWS_OUT:] = (both[ROWS_OUT:] + parts).astype(bf16)
        return 0

    lax.fori_loop(0, 16, step, 0)


def slab_rows(core):
    zh = lax.axis_index("zh")
    for x in range(4):
        for y in range(4):
            for z in (zh, 1 - zh):
                slab = ((x * 2 + z) * 4 + y) * 2 + core
                yield pl.ds(pl.multiple_of(slab * 16, 16), 16)


def dot_slabs(left, slabs, core):
    picked = jnp.concatenate([left[rows, :] for rows in slab_rows(core)], axis=0)
    return dot(picked, slabs[...].reshape(512, 1024), 0, 0)


def rotate_kernel(slabs, grad, rotated):
    rotated[...] = dot_slabs(grad, slabs, lax.axis_index("core"))


def scale_kernel(slabs, grad, partial, q_out, values_in, values_out, back, inner_out):
    total = partial[...] + dot_slabs(grad, slabs, 1 - lax.axis_index("core"))
    q = q_out[...]
    spectral = dot(q, total.astype(bf16), 0, 0)
    scaled = (spectral / (values_in[...] * values_out[...] + damping)).astype(bf16)
    back_rot = dot(q, scaled, 1, 0).astype(bf16)
    back[...] = back_rot
    inner = jnp.sum(
        jnp.sum(back_rot.astype(f32) * total, axis=0, keepdims=True), axis=1, keepdims=True
    )
    inner_out[...] = jnp.broadcast_to(inner, (8, 128))


def finish_kernel(q_own, q_other, back, precond):
    core = lax.axis_index("core")
    for src, c in ((q_own, core), (q_other, 1 - core)):
        result = dot(src[...].reshape(512, 1024), back[...], 1, 1)
        for s, rows in enumerate(slab_rows(c)):
            precond[rows, :] = result[s * 16 : s * 16 + 16]


def clip_kernel(scalars, column, precond, cov_out, update):
    total = jnp.sum(column[...], axis=0)
    cov_out[0] = total[0:32] / scalars[0]
    rate = scalars[1]
    update[...] = jnp.minimum(1.0, jnp.sqrt(kl_clip / (rate * rate * total[32:33]))) * precond[...]


def on_chip(kernel, outs, flops, *args):
    whole = pl.BlockSpec(memory_space=pltpu.VMEM)
    size = sum(a.size * a.dtype.itemsize for a in args)
    return pl.pallas_call(
        kernel,
        in_specs=[whole if a.ndim > 1 else pl.BlockSpec(memory_space=pltpu.SMEM) for a in args],
        out_specs=[whole] * len(outs),
        out_shape=outs,
        compiler_params=pltpu.CompilerParams(vmem_limit_bytes=VMEM),
        cost_estimate=pl.CostEstimate(flops=flops, bytes_accessed=size, transcendentals=0),
        name=kernel.__name__[:-7],
    )(*args)


def total(msg, at, rows):
    out = msg[0, at : at + rows].astype(f32)
    for s in range(1, 16):
        out = out + msg[s, at : at + rows].astype(f32)
    return out


def unpack_in_kernel(msg, keep, send):
    first = lax.axis_index("zh") == 0
    for c in range(8):
        pair = total(msg, c * 32, 32)
        low, high = pair[:16], pair[16:]
        keep[:, c * 128 : c * 128 + 128] = jnp.where(first, low, high)
        send[:, c * 128 : c * 128 + 128] = jnp.where(first, high, low)


def unpack_out_kernel(msg, column):
    folded = total(msg, 0, ROWS_OUT)
    extra = total(msg, ROWS_OUT, ROWS_EXTRA)
    turned = folded.T
    row = lax.broadcasted_iota(jnp.int32, (128, 128), 0)
    col = lax.broadcasted_iota(jnp.int32, (128, 128), 1)
    one = jnp.where(row <= col, folded, turned)
    two = jnp.where(row > col, folded, jnp.where(row == col, extra[0:1], turned))
    inner = jnp.broadcast_to(extra[1:2] + extra[2:3] + extra[3:4], (8, 128))
    for z in range(4):
        column[z, 0:32] = one[z * 32 : z * 32 + 32]
        column[4 + z, 0:32] = two[z * 32 : z * 32 + 32]
        column[z, 32:40] = inner
        column[4 + z, 32:40] = inner


def swap(array, axis):
    return lax.ppermute(array, axis, [(0, 1), (1, 0)])


def local(
    activations,
    output_grads,
    token_counts,
    owner_blocks,
    basis_in,
    basis_out,
    values_in,
    values_out,
    gradient,
    learning_rate,
):
    token_total = jnp.sum(token_counts).astype(f32)
    shape = jax.ShapeDtypeStruct
    core = lax.axis_index("core").astype(jnp.int32)[None]
    mine = basis_in[0]
    slabs = jnp.concatenate([mine, swap(mine, "zh")], axis=0)
    send_in, keep_in = cov_in_partial(activations, token_counts)
    slabs, send_in, counts = lax.optimization_barrier((slabs, send_in, token_counts))
    recv_in = swap(send_in, "core")
    q_own = lax.all_to_all(
        jnp.broadcast_to(slabs[None], (16,) + slabs.shape), PLANE, 0, 0, tiled=True
    )
    send_out, keep_out = cov_out_partial(output_grads, owner_blocks, counts, core)
    recv_out = swap(send_out, "core")
    (msg_in,) = on_chip(pack_in_kernel, [shape((16, ROWS_IN, 128), bf16)], 1024, keep_in, recv_in)
    q_own, msg_in, keep_out = lax.optimization_barrier((q_own, msg_in, keep_out))
    got_in = lax.all_to_all(msg_in, PLANE, 0, 0, tiled=True)
    q_other = swap(q_own, "core")
    (partial,) = on_chip(rotate_kernel, [shape((128, 1024), f32)], 1024, q_own, gradient)
    back, inner = on_chip(
        scale_kernel,
        [shape((128, 1024), bf16), shape((8, 128), f32)],
        1024,
        q_other,
        gradient,
        partial,
        basis_out[0],
        values_in[None, :],
        values_out[:, None],
    )
    (msg_out,) = on_chip(
        pack_out_kernel,
        [shape((16, ROWS_OUT + ROWS_EXTRA, 128), bf16)],
        1024,
        keep_out,
        recv_out,
        inner,
        swap(inner, "core"),
    )
    got_in, msg_out = lax.optimization_barrier((got_in, msg_out))
    got_out = lax.all_to_all(msg_out, PLANE, 0, 0, tiled=True)
    keep_slab, send_slab = on_chip(unpack_in_kernel, [shape((16, 1024), f32)] * 2, 1024, got_in)
    recv_slab = swap(send_slab, "zh")
    (column,) = on_chip(unpack_out_kernel, [shape((8, 40, 128), f32)], 1024, got_out)
    column, recv_slab = lax.optimization_barrier((column, recv_slab))
    column = lax.all_to_all(column, COLUMN, 0, 0, tiled=True)
    (precond,) = on_chip(finish_kernel, [shape((1024, 128), f32)], 1024, q_own, q_other, back)
    cov_in = ((keep_slab + recv_slab) / token_total)[None]
    cov_out, update = on_chip(
        clip_kernel,
        [shape((1, 32, 128), f32), shape((1024, 128), f32)],
        1 << 20,
        jnp.stack([token_total, learning_rate[0]]),
        column,
        precond,
    )
    return (cov_in, cov_out, update)


def solution(mesh):
    fine = Mesh(mesh.devices.reshape(SIZES), AXES)
    placed = (
        P(DP, "zl"),
        P(AXES, None),
        P(),
        P(),
        P("zl", DP, None),
        P(DP, None, None),
        P("zl"),
        P(DP),
        P("zl", DP),
        P(),
    )
    return jax.shard_map(
        local,
        mesh=fine,
        in_specs=placed,
        out_specs=(P("zl", DP, None), P(DP, "zl", None), P("zl", DP)),
        check_vma=False,
    )
```

```python
import jax
import jax.numpy as jnp
from jax import lax
from jax.experimental import pallas as pl
from jax.experimental.pallas import tpu as pltpu
from jax.sharding import Mesh, PartitionSpec as P

damping = 0.03
kl_clip = 0.001
f32 = jnp.float32
bf16 = jnp.bfloat16

AXES = ("x", "zh", "y", "core", "zl")
SIZES = (4, 2, 4, 2, 4)
DP = ("x", "zh", "y", "core")
PLANE = ("x", "y")
COLUMN = ("zh", "zl")
VMEM = 20 << 20

ROWS_IN = 256
ROWS_OUT = 128
ROWS_EXTRA = 16
ROWS = ROWS_IN + ROWS_OUT + ROWS_EXTRA


def dot(a, b, ca, cb):
    return lax.dot_general(a, b, (((ca,), (cb,)), ((), ())), preferred_element_type=f32)


def counted():
    core = lax.axis_index("core")
    dp = ((lax.axis_index("x") * 2 + lax.axis_index("zh")) * 4 + lax.axis_index("y")) * 2 + core
    return dp, core, lax.axis_index("zl")


def cov_out_kernel(owners, counts, core, *refs):
    blocks, (send, keep) = refs[:8], refs[8:]
    dp, _, zl = counted()
    quarter = blocks[0].shape[0]
    live = counts[dp] - zl * quarter
    rows = lax.broadcasted_iota(jnp.int32, blocks[0].shape, 0) < live
    row = lax.broadcasted_iota(jnp.int32, (128, 128), 0)
    col = lax.broadcasted_iota(jnp.int32, (128, 128), 1)
    top = lax.broadcasted_iota(jnp.int32, (ROWS_EXTRA, 128), 0) == 0

    rows = jnp.concatenate([rows, rows], axis=1)
    for y in range(2):
        for at, dst in ((0, keep), (4, send)):
            full = jnp.concatenate([blocks[at + y][...], blocks[at + 2 + y][...]], axis=1)
            both = dot(jnp.where(rows, full, jnp.zeros((), bf16)), full, 0, 0)
            first, second = both[:128, :128], both[128:, 128:]
            diag = jnp.sum(jnp.where(row == col, second, 0.0), axis=0, keepdims=True)
            dst[y, 0:ROWS_OUT] = jnp.where(row <= col, first, second).astype(dst.dtype)
            dst[y, ROWS_OUT:] = jnp.where(top, diag, 0.0).astype(dst.dtype)


def cov_out_partial(output_grads, owners, counts, core):
    quarter = output_grads.shape[0]

    def at(zh, y, other):
        def index(s, owners, counts, core):
            c = 1 - core[0] if other else core[0]
            x, half = s // 2, s % 2
            return (0, owners[((x * 2 + zh) * 4 + half * 2 + y) * 2 + c])

        return pl.BlockSpec((quarter, 128), index)

    rows = ROWS_OUT + ROWS_EXTRA
    out = pl.BlockSpec((2, rows, 128), lambda s, *_: (s, 0, 0))
    order = [(zh, y, other) for other in (False, True) for zh in range(2) for y in range(2)]
    return pl.pallas_call(
        cov_out_kernel,
        grid_spec=pltpu.PrefetchScalarGridSpec(
            num_scalar_prefetch=3,
            grid=(8,),
            in_specs=[at(*o) for o in order],
            out_specs=[out, out],
        ),
        out_shape=[
            jax.ShapeDtypeStruct((16, rows, 128), bf16),
            jax.ShapeDtypeStruct((16, rows, 128), f32),
        ],
        compiler_params=pltpu.CompilerParams(vmem_limit_bytes=VMEM),
        cost_estimate=pl.CostEstimate(
            flops=2 * quarter * 8192 * 128, bytes_accessed=quarter * 8192 * 2 + (4 << 20), transcendentals=0
        ),
        name="cov_out_partial",
    )(owners, counts, core, *([output_grads] * 8))


def cov_in_kernel(counts, lhs, rhs, send, keep):
    dp, core, _ = counted()
    first = core == 0
    rows = lax.broadcasted_iota(jnp.int32, lhs.shape, 0) < counts[dp]
    masked = jnp.where(rows, lhs[...], jnp.zeros((), bf16))
    part = dot(masked, rhs[...], 0, 0)
    for zh in range(2):
        for y in range(4):
            at = (zh * 4 + y) * 32
            low, high = part[at : at + 16], part[at + 16 : at + 32]
            for dst, rows in (
                (keep, jnp.where(first, low, high)),
                (send, jnp.where(first, high, low).astype(bf16)),
            ):
                for c in range(8):
                    at = c * 32 + zh * 16
                    dst[y, at : at + 16] = rows[:, c * 128 : c * 128 + 128]


def cov_in_partial(activations, counts):
    tok = activations.shape[0]
    out = pl.BlockSpec((4, ROWS_IN, 128), lambda s, *_: (s, 0, 0))
    return pl.pallas_call(
        cov_in_kernel,
        grid_spec=pltpu.PrefetchScalarGridSpec(
            num_scalar_prefetch=1,
            grid=(4,),
            in_specs=[
                pl.BlockSpec((tok, 256), lambda s, *_: (0, s)),
                pl.BlockSpec((tok, 1024), lambda s, *_: (0, 0)),
            ],
            out_specs=[out, out],
        ),
        out_shape=[
            jax.ShapeDtypeStruct((16, ROWS_IN, 128), bf16),
            jax.ShapeDtypeStruct((16, ROWS_IN, 128), f32),
        ],
        compiler_params=pltpu.CompilerParams(vmem_limit_bytes=VMEM),
        cost_estimate=pl.CostEstimate(
            flops=2 * tok * 1024 * 1024, bytes_accessed=tok * 4096 + (4 << 20), transcendentals=0
        ),
        name="cov_in_partial",
    )(counts, activations, activations)


def pack_kernel(keep_in, recv_in, keep_out, recv_out, msg):
    def step(s, _):
        msg[s, 0:ROWS_IN] = (keep_in[s] + recv_in[s].astype(f32)).astype(bf16)
        msg[s, ROWS_IN:] = (keep_out[s] + recv_out[s].astype(f32)).astype(bf16)
        return 0

    lax.fori_loop(0, 16, step, 0)


def slab_rows(core):
    x, zh = lax.axis_index("x"), lax.axis_index("zh")
    for y in range(4):
        for step in range(4):
            for z in (zh, 1 - zh):
                slab = ((lax.rem(x + 4 - step, 4) * 2 + z) * 4 + y) * 2 + core
                yield pl.ds(pl.multiple_of(slab * 16, 16), 16)


def dot_slabs(left, slabs, core):
    picked = jnp.concatenate([left[rows, :] for rows in slab_rows(core)], axis=0)
    return dot(picked, slabs[...].reshape(512, 1024), 0, 0)


def rotate_kernel(slabs, grad, rotated):
    rotated[...] = dot_slabs(grad, slabs, lax.axis_index("core"))


def scale_kernel(slabs, grad, partial, q_out, values_in, values_out, back, inner_out):
    total = partial[...] + dot_slabs(grad, slabs, 1 - lax.axis_index("core"))
    q = q_out[...]
    spectral = dot(q, total.astype(bf16), 0, 0)
    scaled = (spectral / (values_in[...] * values_out[...] + damping)).astype(bf16)
    back_rot = dot(q, scaled, 1, 0).astype(bf16)
    back[...] = back_rot
    inner = jnp.sum(
        jnp.sum(back_rot.astype(f32) * total, axis=0, keepdims=True), axis=1, keepdims=True
    )
    inner_out[...] = jnp.broadcast_to(inner, (8, 128))


def finish_kernel(q_own, q_other, back, precond):
    core = lax.axis_index("core")
    for src, c in ((q_own, core), (q_other, 1 - core)):
        result = dot(src[...].reshape(512, 1024), back[...], 1, 1)
        for s, rows in enumerate(slab_rows(c)):
            precond[rows, :] = result[s * 16 : s * 16 + 16]


def clip_kernel(scalars, column, precond, cov_out, update):
    total = jnp.sum(column[...], axis=0)
    cov_out[0] = total[0:32] / scalars[0]
    rate = scalars[1]
    update[...] = jnp.minimum(1.0, jnp.sqrt(kl_clip / (rate * rate * total[32:33]))) * precond[...]


def on_chip(kernel, outs, flops, *args):
    whole = pl.BlockSpec(memory_space=pltpu.VMEM)
    size = sum(a.size * a.dtype.itemsize for a in args)
    return pl.pallas_call(
        kernel,
        in_specs=[whole if a.ndim > 1 else pl.BlockSpec(memory_space=pltpu.SMEM) for a in args],
        out_specs=[whole] * len(outs),
        out_shape=outs,
        compiler_params=pltpu.CompilerParams(vmem_limit_bytes=VMEM),
        cost_estimate=pl.CostEstimate(flops=flops, bytes_accessed=size, transcendentals=0),
        name=kernel.__name__[:-7],
    )(*args)


def total(msg, at, rows):
    out = msg[0, at : at + rows].astype(f32)
    for s in range(1, 16):
        out = out + msg[s, at : at + rows].astype(f32)
    return out


def unpack_kernel(msg, keep, send, column):
    first = lax.axis_index("zh") == 0
    for c in range(8):
        pair = total(msg, c * 32, 32)
        low, high = pair[:16], pair[16:]
        keep[:, c * 128 : c * 128 + 128] = jnp.where(first, low, high)
        send[:, c * 128 : c * 128 + 128] = jnp.where(first, high, low)
    folded = total(msg, ROWS_IN, ROWS_OUT)
    diag = total(msg, ROWS_IN + ROWS_OUT, ROWS_EXTRA)[0:1]
    turned = folded.T
    row = lax.broadcasted_iota(jnp.int32, (128, 128), 0)
    col = lax.broadcasted_iota(jnp.int32, (128, 128), 1)
    one = jnp.where(row <= col, folded, turned)
    two = jnp.where(row > col, folded, jnp.where(row == col, diag, turned))
    for z in range(4):
        column[z] = one[z * 32 : z * 32 + 32]
        column[4 + z] = two[z * 32 : z * 32 + 32]


def join_kernel(column, inner, joined):
    total = jnp.sum(inner[...], axis=0)
    for z in range(8):
        joined[z, 0:32] = column[z]
        joined[z, 32:40] = total


def swap(array, axis):
    return lax.ppermute(array, axis, [(0, 1), (1, 0)])


def local(
    activations,
    output_grads,
    token_counts,
    owner_blocks,
    basis_in,
    basis_out,
    values_in,
    values_out,
    gradient,
    learning_rate,
):
    token_total = jnp.sum(token_counts).astype(f32)
    shape = jax.ShapeDtypeStruct
    core = lax.axis_index("core").astype(jnp.int32)[None]
    mine = basis_in[0]
    slabs = jnp.concatenate([mine, swap(mine, "zh")], axis=0)
    send_in, keep_in = cov_in_partial(activations, token_counts)
    slabs, send_in, counts = lax.optimization_barrier((slabs, send_in, token_counts))
    slabs = [slabs] + [
        lax.ppermute(slabs, "x", [(j, (j + step) % 4) for j in range(4)]) for step in (1, 2, 3)
    ]
    recv_in = swap(send_in, "core")
    send_out, keep_out = cov_out_partial(output_grads, owner_blocks, counts, core)
    slabs, send_out, recv_in = lax.optimization_barrier(
        (jnp.concatenate(slabs, axis=0), send_out, recv_in)
    )
    q_own = lax.all_gather(slabs, "y", axis=0, tiled=False)
    recv_out = swap(send_out, "core")
    (msg,) = on_chip(
        pack_kernel, [shape((16, ROWS, 128), bf16)], 1024, keep_in, recv_in, keep_out, recv_out
    )
    msg = lax.all_to_all(msg, PLANE, 0, 0, tiled=True)
    q_other = swap(q_own, "core")
    (partial,) = on_chip(rotate_kernel, [shape((128, 1024), f32)], 1024, q_own, gradient)
    back, inner = on_chip(
        scale_kernel,
        [shape((128, 1024), bf16), shape((8, 128), f32)],
        1024,
        q_other,
        gradient,
        partial,
        basis_out[0],
        values_in[None, :],
        values_out[:, None],
    )
    msg, inner = lax.optimization_barrier((msg, inner))
    inner = lax.all_to_all(
        jnp.broadcast_to(inner[None], (32, 8, 128)), ("x", "y", "core"), 0, 0, tiled=True
    )
    keep_slab, send_slab, column = on_chip(
        unpack_kernel,
        [shape((16, 1024), f32), shape((16, 1024), f32), shape((8, 32, 128), f32)],
        1024,
        msg,
    )
    recv_slab = swap(send_slab, "zh")
    (column,) = on_chip(join_kernel, [shape((8, 40, 128), f32)], 1024, column, inner)
    column, recv_slab = lax.optimization_barrier((column, recv_slab))
    column = lax.all_to_all(column, COLUMN, 0, 0, tiled=True)
    (precond,) = on_chip(finish_kernel, [shape((1024, 128), f32)], 1024, q_own, q_other, back)
    cov_in = ((keep_slab + recv_slab) / token_total)[None]
    cov_out, update = on_chip(
        clip_kernel,
        [shape((1, 32, 128), f32), shape((1024, 128), f32)],
        1 << 20,
        jnp.stack([token_total, learning_rate[0]]),
        column,
        precond,
    )
    return (cov_in, cov_out, update)


def solution(mesh):
    fine = Mesh(mesh.devices.reshape(SIZES), AXES)
    placed = (
        P(DP, "zl"),
        P(AXES, None),
        P(),
        P(),
        P("zl", DP, None),
        P(DP, None, None),
        P("zl"),
        P(DP),
        P("zl", DP),
        P(),
    )
    return jax.shard_map(
        local,
        mesh=fine,
        in_specs=placed,
        out_specs=(P("zl", DP, None), P(DP, "zl", None), P("zl", DP)),
        check_vma=False,
    )
```

```python
import jax
import jax.numpy as jnp
from jax import lax
from jax.experimental import pallas as pl
from jax.experimental.pallas import tpu as pltpu
from jax.sharding import Mesh, PartitionSpec as P

damping = 0.03
kl_clip = 0.001
f32 = jnp.float32
bf16 = jnp.bfloat16

AXES = ("x", "zh", "y", "core", "zl")
SIZES = (4, 2, 4, 2, 4)
DP = ("x", "zh", "y", "core")
PLANE = ("x", "y")
COLUMN = ("zh", "zl")
VMEM = 20 << 20

ROWS_OUT = 128
ROWS_EXTRA = 16


def dot(a, b, ca, cb):
    return lax.dot_general(a, b, (((ca,), (cb,)), ((), ())), preferred_element_type=f32)


def counted():
    core = lax.axis_index("core")
    dp = ((lax.axis_index("x") * 2 + lax.axis_index("zh")) * 4 + lax.axis_index("y")) * 2 + core
    return dp, core, lax.axis_index("zl")


def cov_out_kernel(owners, counts, core, *refs):
    blocks, (send, keep) = refs[:8], refs[8:]
    dp, _, zl = counted()
    quarter = blocks[0].shape[0]
    live = counts[dp] - zl * quarter
    rows = lax.broadcasted_iota(jnp.int32, blocks[0].shape, 0) < live
    row = lax.broadcasted_iota(jnp.int32, (128, 128), 0)
    col = lax.broadcasted_iota(jnp.int32, (128, 128), 1)
    top = lax.broadcasted_iota(jnp.int32, (ROWS_EXTRA, 128), 0) == 0

    rows = jnp.concatenate([rows, rows], axis=1)
    for y in range(2):
        for at, dst in ((0, keep), (4, send)):
            full = jnp.concatenate([blocks[at + y][...], blocks[at + 2 + y][...]], axis=1)
            both = dot(jnp.where(rows, full, jnp.zeros((), bf16)), full, 0, 0)
            first, second = both[:128, :128], both[128:, 128:]
            diag = jnp.sum(jnp.where(row == col, second, 0.0), axis=0, keepdims=True)
            dst[y, 0:ROWS_OUT] = jnp.where(row <= col, first, second).astype(dst.dtype)
            dst[y, ROWS_OUT:] = jnp.where(top, diag, 0.0).astype(dst.dtype)


def cov_out_partial(output_grads, owners, counts, core):
    quarter = output_grads.shape[0]

    def at(zh, y, other):
        def index(s, owners, counts, core):
            c = 1 - core[0] if other else core[0]
            x, half = s // 2, s % 2
            return (0, owners[((x * 2 + zh) * 4 + half * 2 + y) * 2 + c])

        return pl.BlockSpec((quarter, 128), index)

    rows = ROWS_OUT + ROWS_EXTRA
    out = pl.BlockSpec((2, rows, 128), lambda s, *_: (s, 0, 0))
    order = [(zh, y, other) for other in (False, True) for zh in range(2) for y in range(2)]
    return pl.pallas_call(
        cov_out_kernel,
        grid_spec=pltpu.PrefetchScalarGridSpec(
            num_scalar_prefetch=3,
            grid=(8,),
            in_specs=[at(*o) for o in order],
            out_specs=[out, out],
        ),
        out_shape=[
            jax.ShapeDtypeStruct((16, rows, 128), bf16),
            jax.ShapeDtypeStruct((16, rows, 128), f32),
        ],
        compiler_params=pltpu.CompilerParams(vmem_limit_bytes=VMEM),
        cost_estimate=pl.CostEstimate(
            flops=2 * quarter * 8192 * 128, bytes_accessed=quarter * 8192 * 2 + (4 << 20), transcendentals=0
        ),
        name="cov_out_partial",
    )(owners, counts, core, *([output_grads] * 8))


def cov_in_kernel(counts, tokens, send, keep):
    dp, core, _ = counted()
    first = core == 0
    start = pl.multiple_of(pl.program_id(0) * 256, 256)
    some = tokens[:, pl.ds(start, 256)]
    live = lax.broadcasted_iota(jnp.int32, some.shape, 0) < counts[dp]
    part = dot(jnp.where(live, some, jnp.zeros((), bf16)), tokens[...], 0, 0)
    for zh in range(2):
        for y in range(4):
            at = (zh * 4 + y) * 32
            low, high = part[at : at + 16], part[at + 16 : at + 32]
            keep[y, zh * 16 : zh * 16 + 16] = jnp.where(first, low, high)
            send[y, zh * 16 : zh * 16 + 16] = jnp.where(first, high, low).astype(bf16)


def cov_in_partial(activations, counts):
    tok = activations.shape[0]
    out = pl.BlockSpec((4, 32, 1024), lambda s, *_: (s, 0, 0))
    return pl.pallas_call(
        cov_in_kernel,
        grid_spec=pltpu.PrefetchScalarGridSpec(
            num_scalar_prefetch=1,
            grid=(4,),
            in_specs=[pl.BlockSpec((tok, 1024), lambda s, *_: (0, 0))],
            out_specs=[out, out],
        ),
        out_shape=[
            jax.ShapeDtypeStruct((16, 32, 1024), bf16),
            jax.ShapeDtypeStruct((16, 32, 1024), f32),
        ],
        compiler_params=pltpu.CompilerParams(vmem_limit_bytes=60 << 20),
        cost_estimate=pl.CostEstimate(
            flops=2 * tok * 1024 * 1024, bytes_accessed=tok * 4096 + (4 << 20), transcendentals=0
        ),
        name="cov_in_partial",
    )(counts, activations)


def pack_in_kernel(mine, pair, keep, recv, msg):
    for s in range(msg.shape[0]):
        msg[s, 0:16] = mine[...]
        msg[s, 16:32] = pair[...]
        msg[s, 32:64] = (keep[s] + recv[s].astype(f32)).astype(bf16)


def pack_out_kernel(keep, recv, inner, other_inner, msg):
    total = inner[0:1] + other_inner[0:1]
    high = total.astype(bf16).astype(f32)
    rest = total - high
    middle = rest.astype(bf16).astype(f32)
    low = rest - middle
    row = lax.broadcasted_iota(jnp.int32, (ROWS_EXTRA, 128), 0)
    parts = jnp.where(
        row == 1, high, jnp.where(row == 2, middle, jnp.where(row == 3, low, 0.0))
    )
    for s in range(msg.shape[0]):
        both = keep[s] + recv[s].astype(f32)
        msg[s, 0:ROWS_OUT] = both[0:ROWS_OUT].astype(bf16)
        msg[s, ROWS_OUT:] = (both[ROWS_OUT:] + parts).astype(bf16)


def streamed(kernel, steps, out, *args):
    def spec(a):
        if a.shape[0] == 16 and a.ndim == 3:
            return pl.BlockSpec((16 // steps,) + a.shape[1:], lambda s: (s, 0, 0))
        return pl.BlockSpec(a.shape, lambda s: (0,) * a.ndim)

    return pl.pallas_call(
        kernel,
        grid=(steps,),
        in_specs=[spec(a) for a in args],
        out_specs=spec(out),
        out_shape=out,
        compiler_params=pltpu.CompilerParams(vmem_limit_bytes=52 << 20),
        cost_estimate=pl.CostEstimate(flops=1024, bytes_accessed=1024, transcendentals=0),
        name=kernel.__name__[:-7],
    )(*args)


def slab_rows(core):
    zh = lax.axis_index("zh")
    for x in range(4):
        for y in range(4):
            for z in (zh, 1 - zh):
                slab = ((x * 2 + z) * 4 + y) * 2 + core
                yield pl.ds(pl.multiple_of(slab * 16, 16), 16)


def dot_slabs(left, slabs, core):
    picked = jnp.concatenate([left[rows, :] for rows in slab_rows(core)], axis=0)
    return dot(picked, slabs[...].reshape(512, 1024), 0, 0)


def rotate_kernel(slabs, grad, rotated):
    rotated[...] = dot_slabs(grad, slabs, lax.axis_index("core"))


def scale_kernel(slabs, grad, partial, q_out, values_in, values_out, back, inner_out):
    total = partial[...] + dot_slabs(grad, slabs, 1 - lax.axis_index("core"))
    q = q_out[...]
    spectral = dot(q, total.astype(bf16), 0, 0)
    scaled = (spectral / (values_in[...] * values_out[...] + damping)).astype(bf16)
    back_rot = dot(q, scaled, 1, 0).astype(bf16)
    back[...] = back_rot
    inner = jnp.sum(
        jnp.sum(back_rot.astype(f32) * total, axis=0, keepdims=True), axis=1, keepdims=True
    )
    inner_out[...] = jnp.broadcast_to(inner, (8, 128))


def finish_kernel(q_own, q_other, back, precond):
    core = lax.axis_index("core")
    for src, c in ((q_own, core), (q_other, 1 - core)):
        result = dot(src[...].reshape(512, 1024), back[...], 1, 1)
        for s, rows in enumerate(slab_rows(c)):
            precond[rows, :] = result[s * 16 : s * 16 + 16]


def clip_kernel(scalars, column, precond, cov_out, update):
    total = jnp.sum(column[...], axis=0)
    cov_out[0] = total[0:32] / scalars[0]
    rate = scalars[1]
    update[...] = jnp.minimum(1.0, jnp.sqrt(kl_clip / (rate * rate * total[32:33]))) * precond[...]


def on_chip(kernel, outs, flops, *args):
    whole = pl.BlockSpec(memory_space=pltpu.VMEM)
    size = sum(a.size * a.dtype.itemsize for a in args)
    return pl.pallas_call(
        kernel,
        in_specs=[whole if a.ndim > 1 else pl.BlockSpec(memory_space=pltpu.SMEM) for a in args],
        out_specs=[whole] * len(outs),
        out_shape=outs,
        compiler_params=pltpu.CompilerParams(vmem_limit_bytes=VMEM),
        cost_estimate=pl.CostEstimate(flops=flops, bytes_accessed=size, transcendentals=0),
        name=kernel.__name__[:-7],
    )(*args)


def total(msg, at, rows):
    out = msg[0, at : at + rows].astype(f32)
    for s in range(1, 16):
        out = out + msg[s, at : at + rows].astype(f32)
    return out


def unpack_in_kernel(msg, keep, send):
    first = lax.axis_index("zh") == 0
    pair = total(msg, 32, 32)
    low, high = pair[:16], pair[16:]
    keep[...] = jnp.where(first, low, high)
    send[...] = jnp.where(first, high, low)


def unpack_out_kernel(msg, column):
    folded = total(msg, 0, ROWS_OUT)
    extra = total(msg, ROWS_OUT, ROWS_EXTRA)
    turned = folded.T
    row = lax.broadcasted_iota(jnp.int32, (128, 128), 0)
    col = lax.broadcasted_iota(jnp.int32, (128, 128), 1)
    one = jnp.where(row <= col, folded, turned)
    two = jnp.where(row > col, folded, jnp.where(row == col, extra[0:1], turned))
    inner = jnp.broadcast_to(extra[1:2] + extra[2:3] + extra[3:4], (8, 128))
    for z in range(4):
        column[z, 0:32] = one[z * 32 : z * 32 + 32]
        column[4 + z, 0:32] = two[z * 32 : z * 32 + 32]
        column[z, 32:40] = inner
        column[4 + z, 32:40] = inner


def swap(array, axis):
    return lax.ppermute(array, axis, [(0, 1), (1, 0)])


def local(
    activations,
    output_grads,
    token_counts,
    owner_blocks,
    basis_in,
    basis_out,
    values_in,
    values_out,
    gradient,
    learning_rate,
):
    token_total = jnp.sum(token_counts).astype(f32)
    shape = jax.ShapeDtypeStruct
    core = lax.axis_index("core").astype(jnp.int32)[None]
    mine = basis_in[0]
    pair = swap(mine, "zh")
    send_in, keep_in = cov_in_partial(activations, token_counts)
    pair, send_in = lax.optimization_barrier((pair, send_in))
    recv_in = swap(send_in, "core")
    msg_in = streamed(
        pack_in_kernel, 4, shape((16, 64, 1024), bf16), mine, pair, keep_in, recv_in
    )
    msg_in, counts = lax.optimization_barrier((msg_in, token_counts))
    got_in = lax.all_to_all(msg_in, PLANE, 0, 0, tiled=True)
    send_out, keep_out = cov_out_partial(output_grads, owner_blocks, counts, core)
    recv_out = swap(send_out, "core")
    got_in, keep_out, recv_out = lax.optimization_barrier((got_in, keep_out, recv_out))
    q_own = got_in[:, :32]
    q_other = swap(q_own, "core")
    (partial,) = on_chip(rotate_kernel, [shape((128, 1024), f32)], 1024, q_own, gradient)
    back, inner = on_chip(
        scale_kernel,
        [shape((128, 1024), bf16), shape((8, 128), f32)],
        1024,
        q_other,
        gradient,
        partial,
        basis_out[0],
        values_in[None, :],
        values_out[:, None],
    )
    (precond,) = on_chip(finish_kernel, [shape((1024, 128), f32)], 1024, q_own, q_other, back)
    other_inner, precond = lax.optimization_barrier((swap(inner, "core"), precond))
    msg_out = streamed(
        pack_out_kernel,
        2,
        shape((16, ROWS_OUT + ROWS_EXTRA, 128), bf16),
        keep_out,
        recv_out,
        inner,
        other_inner,
    )
    got_in, msg_out = lax.optimization_barrier((got_in, msg_out))
    got_out = lax.all_to_all(msg_out, PLANE, 0, 0, tiled=True)
    keep_slab, send_slab = on_chip(unpack_in_kernel, [shape((16, 1024), f32)] * 2, 1024, got_in)
    recv_slab = swap(send_slab, "zh")
    (column,) = on_chip(unpack_out_kernel, [shape((8, 40, 128), f32)], 1024, got_out)
    column, recv_slab = lax.optimization_barrier((column, recv_slab))
    column = lax.all_to_all(column, COLUMN, 0, 0, tiled=True)
    cov_in = ((keep_slab + recv_slab) / token_total)[None]
    cov_out, update = on_chip(
        clip_kernel,
        [shape((1, 32, 128), f32), shape((1024, 128), f32)],
        1 << 20,
        jnp.stack([token_total, learning_rate[0]]),
        column,
        precond,
    )
    return (cov_in, cov_out, update)


def solution(mesh):
    fine = Mesh(mesh.devices.reshape(SIZES), AXES)
    placed = (
        P(DP, "zl"),
        P(AXES, None),
        P(),
        P(),
        P("zl", DP, None),
        P(DP, None, None),
        P("zl"),
        P(DP),
        P("zl", DP),
        P(),
    )
    return jax.shard_map(
        local,
        mesh=fine,
        in_specs=placed,
        out_specs=(P("zl", DP, None), P(DP, "zl", None), P("zl", DP)),
        check_vma=False,
    )
```

```python
import jax
import jax.numpy as jnp
from jax import lax
from jax.experimental import pallas as pl
from jax.experimental.pallas import tpu as pltpu
from jax.sharding import Mesh, PartitionSpec as P

damping = 0.03
kl_clip = 0.001
f32 = jnp.float32
bf16 = jnp.bfloat16

AXES = ("x", "zh", "y", "core", "zl")
SIZES = (4, 2, 4, 2, 4)
DP = ("x", "zh", "y", "core")
PLANE = ("x", "y")
COLUMN = ("zh", "zl")
VMEM = 20 << 20

ROWS_OUT = 128
ROWS_EXTRA = 16


def dot(a, b, ca, cb):
    return lax.dot_general(a, b, (((ca,), (cb,)), ((), ())), preferred_element_type=f32)


def counted():
    core = lax.axis_index("core")
    dp = ((lax.axis_index("x") * 2 + lax.axis_index("zh")) * 4 + lax.axis_index("y")) * 2 + core
    return dp, core, lax.axis_index("zl")


def cov_out_kernel(owners, counts, tokens, send, keep):
    dp, core, zl = counted()
    quarter = tokens.shape[0]
    live = counts[dp] - zl * quarter
    live = lax.broadcasted_iota(jnp.int32, (quarter, 256), 0) < live
    row = lax.broadcasted_iota(jnp.int32, (128, 128), 0)
    col = lax.broadcasted_iota(jnp.int32, (128, 128), 1)
    top = lax.broadcasted_iota(jnp.int32, (ROWS_EXTRA, 128), 0) == 0

    def block(x, zh, y, c):
        at = owners[((x * 2 + zh) * 4 + y) * 2 + c]
        return tokens[:, pl.ds(pl.multiple_of(at * 128, 128), 128)]

    def step(s, _):
        x, y = s // 4, s % 4
        for c, dst in ((core, keep), (1 - core, send)):
            full = jnp.concatenate([block(x, 0, y, c), block(x, 1, y, c)], axis=1)
            both = dot(jnp.where(live, full, jnp.zeros((), bf16)), full, 0, 0)
            first, second = both[:128, :128], both[128:, 128:]
            diag = jnp.sum(jnp.where(row == col, second, 0.0), axis=0, keepdims=True)
            dst[s, 0:ROWS_OUT] = jnp.where(row <= col, first, second).astype(dst.dtype)
            dst[s, ROWS_OUT:] = jnp.where(top, diag, 0.0).astype(dst.dtype)
        return 0

    lax.fori_loop(0, 16, step, 0, unroll=2)


def cov_in_kernel(counts, tokens, send, keep):
    dp, core, _ = counted()
    first = core == 0
    live = lax.broadcasted_iota(jnp.int32, (tokens.shape[0], 256), 0) < counts[dp]
    for x in range(4):
        some = jnp.where(live, tokens[:, x * 256 : x * 256 + 256], jnp.zeros((), bf16))
        part = dot(some, tokens[...], 0, 0)
        for zh in range(2):
            for y in range(4):
                at = (zh * 4 + y) * 32
                low, high = part[at : at + 16], part[at + 16 : at + 32]
                to = slice(zh * 16, zh * 16 + 16)
                keep[x * 4 + y, to] = jnp.where(first, low, high)
                send[x * 4 + y, to] = jnp.where(first, high, low).astype(bf16)


def pack_in_kernel(keep, recv, msg):
    def step(s, _):
        msg[s] = (keep[s] + recv[s].astype(f32)).astype(bf16)
        return 0

    lax.fori_loop(0, 16, step, 0)


def pack_out_kernel(keep, recv, inner, other_inner, msg):
    total = inner[0:1] + other_inner[0:1]
    high = total.astype(bf16).astype(f32)
    rest = total - high
    middle = rest.astype(bf16).astype(f32)
    low = rest - middle
    row = lax.broadcasted_iota(jnp.int32, (ROWS_EXTRA, 128), 0)
    parts = jnp.where(
        row == 1, high, jnp.where(row == 2, middle, jnp.where(row == 3, low, 0.0))
    )

    def step(s, _):
        both = keep[s] + recv[s].astype(f32)
        msg[s, 0:ROWS_OUT] = both[0:ROWS_OUT].astype(bf16)
        msg[s, ROWS_OUT:] = (both[ROWS_OUT:] + parts).astype(bf16)
        return 0

    lax.fori_loop(0, 16, step, 0)


def slab_rows(core):
    zh = lax.axis_index("zh")
    for x in range(4):
        for y in range(4):
            for z in (zh, 1 - zh):
                slab = ((x * 2 + z) * 4 + y) * 2 + core
                yield pl.ds(pl.multiple_of(slab * 16, 16), 16)


def dot_slabs(left, slabs, core):
    picked = jnp.concatenate([left[rows, :] for rows in slab_rows(core)], axis=0)
    return dot(picked, slabs[...].reshape(512, 1024), 0, 0)


def rotate_kernel(slabs, grad, rotated):
    rotated[...] = dot_slabs(grad, slabs, lax.axis_index("core"))


def scale_kernel(slabs, grad, partial, q_out, values_in, values_out, back, inner_out):
    total = partial[...] + dot_slabs(grad, slabs, 1 - lax.axis_index("core"))
    q = q_out[...]
    spectral = dot(q, total.astype(bf16), 0, 0)
    scaled = (spectral / (values_in[...] * values_out[...] + damping)).astype(bf16)
    back_rot = dot(q, scaled, 1, 0).astype(bf16)
    back[...] = back_rot
    inner = jnp.sum(
        jnp.sum(back_rot.astype(f32) * total, axis=0, keepdims=True), axis=1, keepdims=True
    )
    inner_out[...] = jnp.broadcast_to(inner, (8, 128))


def finish_kernel(q_own, q_other, back, precond):
    core = lax.axis_index("core")
    for src, c in ((q_own, core), (q_other, 1 - core)):
        result = dot(src[...].reshape(512, 1024), back[...], 1, 1)
        for s, rows in enumerate(slab_rows(c)):
            precond[rows, :] = result[s * 16 : s * 16 + 16]


def clip_kernel(scalars, column, precond, cov_out, update):
    total = jnp.sum(column[...], axis=0)
    cov_out[0] = total[0:32] / scalars[0]
    rate = scalars[1]
    update[...] = jnp.minimum(1.0, jnp.sqrt(kl_clip / (rate * rate * total[32:33]))) * precond[...]


def on_chip(kernel, outs, flops, *args):
    whole = pl.BlockSpec(memory_space=pltpu.VMEM)
    size = sum(a.size * a.dtype.itemsize for a in args)
    return pl.pallas_call(
        kernel,
        in_specs=[whole if a.ndim > 1 else pl.BlockSpec(memory_space=pltpu.SMEM) for a in args],
        out_specs=[whole] * len(outs),
        out_shape=outs,
        compiler_params=pltpu.CompilerParams(vmem_limit_bytes=VMEM),
        cost_estimate=pl.CostEstimate(flops=flops, bytes_accessed=size, transcendentals=0),
        name=kernel.__name__[:-7],
    )(*args)


def total(msg, at, rows):
    out = msg[0, at : at + rows].astype(f32)
    for s in range(1, 16):
        out = out + msg[s, at : at + rows].astype(f32)
    return out


def unpack_in_kernel(msg, keep, send):
    first = lax.axis_index("zh") == 0
    pair = total(msg, 0, 32)
    low, high = pair[:16], pair[16:]
    keep[...] = jnp.where(first, low, high)
    send[...] = jnp.where(first, high, low)


def unpack_out_kernel(msg, column):
    folded = total(msg, 0, ROWS_OUT)
    extra = total(msg, ROWS_OUT, ROWS_EXTRA)
    turned = folded.T
    row = lax.broadcasted_iota(jnp.int32, (128, 128), 0)
    col = lax.broadcasted_iota(jnp.int32, (128, 128), 1)
    one = jnp.where(row <= col, folded, turned)
    two = jnp.where(row > col, folded, jnp.where(row == col, extra[0:1], turned))
    inner = jnp.broadcast_to(extra[1:2] + extra[2:3] + extra[3:4], (8, 128))
    for z in range(4):
        column[z, 0:32] = one[z * 32 : z * 32 + 32]
        column[4 + z, 0:32] = two[z * 32 : z * 32 + 32]
        column[z, 32:40] = inner
        column[4 + z, 32:40] = inner


def swap(array, axis):
    return lax.ppermute(array, axis, [(0, 1), (1, 0)])


def local(
    activations,
    output_grads,
    token_counts,
    owner_blocks,
    basis_in,
    basis_out,
    values_in,
    values_out,
    gradient,
    learning_rate,
):
    token_total = jnp.sum(token_counts).astype(f32)
    shape = jax.ShapeDtypeStruct
    mine = basis_in[0]
    slabs = jnp.concatenate([mine, swap(mine, "zh")], axis=0)
    rows = (16, 32, 1024)
    send_in, keep_in = on_chip(
        cov_in_kernel, [shape(rows, bf16), shape(rows, f32)], 2 << 30, token_counts, activations
    )
    slabs, send_in, counts = lax.optimization_barrier((slabs, send_in, token_counts))
    recv_in = swap(send_in, "core")
    q_own = lax.all_to_all(
        jnp.broadcast_to(slabs[None], (16,) + slabs.shape), PLANE, 0, 0, tiled=True
    )
    folded = (16, ROWS_OUT + ROWS_EXTRA, 128)
    send_out, keep_out = on_chip(
        cov_out_kernel,
        [shape(folded, bf16), shape(folded, f32)],
        1 << 30,
        owner_blocks,
        counts,
        output_grads,
    )
    recv_out = swap(send_out, "core")
    (msg_in,) = on_chip(pack_in_kernel, [shape(rows, bf16)], 1024, keep_in, recv_in)
    q_own, msg_in, keep_out = lax.optimization_barrier((q_own, msg_in, keep_out))
    got_in = lax.all_to_all(msg_in, PLANE, 0, 0, tiled=True)
    q_other = swap(q_own, "core")
    (partial,) = on_chip(rotate_kernel, [shape((128, 1024), f32)], 1024, q_own, gradient)
    back, inner = on_chip(
        scale_kernel,
        [shape((128, 1024), bf16), shape((8, 128), f32)],
        1024,
        q_other,
        gradient,
        partial,
        basis_out[0],
        values_in[None, :],
        values_out[:, None],
    )
    (precond,) = on_chip(finish_kernel, [shape((1024, 128), f32)], 1024, q_own, q_other, back)
    other_inner, precond = lax.optimization_barrier((swap(inner, "core"), precond))
    (msg_out,) = on_chip(
        pack_out_kernel,
        [shape(folded, bf16)],
        1024,
        keep_out,
        recv_out,
        inner,
        other_inner,
    )
    got_in, msg_out = lax.optimization_barrier((got_in, msg_out))
    got_out = lax.all_to_all(msg_out, PLANE, 0, 0, tiled=True)
    keep_slab, send_slab = on_chip(unpack_in_kernel, [shape((16, 1024), f32)] * 2, 1024, got_in)
    recv_slab = swap(send_slab, "zh")
    (column,) = on_chip(unpack_out_kernel, [shape((8, 40, 128), f32)], 1024, got_out)
    column, recv_slab = lax.optimization_barrier((column, recv_slab))
    column = lax.all_to_all(column, COLUMN, 0, 0, tiled=True)
    cov_in = ((keep_slab + recv_slab) / token_total)[None]
    cov_out, update = on_chip(
        clip_kernel,
        [shape((1, 32, 128), f32), shape((1024, 128), f32)],
        1 << 20,
        jnp.stack([token_total, learning_rate[0]]),
        column,
        precond,
    )
    return (cov_in, cov_out, update)


def solution(mesh):
    fine = Mesh(mesh.devices.reshape(SIZES), AXES)
    placed = (
        P(DP, "zl"),
        P(AXES, None),
        P(),
        P(),
        P("zl", DP, None),
        P(DP, None, None),
        P("zl"),
        P(DP),
        P("zl", DP),
        P(),
    )
    return jax.shard_map(
        local,
        mesh=fine,
        in_specs=placed,
        out_specs=(P("zl", DP, None), P(DP, "zl", None), P("zl", DP)),
        check_vma=False,
    )
```

```python
import jax
import jax.numpy as jnp
from jax import lax
from jax.experimental import pallas as pl
from jax.experimental.pallas import tpu as pltpu
from jax.sharding import Mesh, PartitionSpec as P

damping = 0.03
kl_clip = 0.001
f32 = jnp.float32
bf16 = jnp.bfloat16

AXES = ("x", "zh", "y", "core", "zl")
SIZES = (4, 2, 4, 2, 4)
DP = ("x", "zh", "y", "core")
PLANE = ("x", "y")
COLUMN = ("zh", "zl")
VMEM = 20 << 20

ROWS_OUT = 128
ROWS_EXTRA = 16


def dot(a, b, ca, cb):
    return lax.dot_general(a, b, (((ca,), (cb,)), ((), ())), preferred_element_type=f32)


def counted():
    core = lax.axis_index("core")
    dp = ((lax.axis_index("x") * 2 + lax.axis_index("zh")) * 4 + lax.axis_index("y")) * 2 + core
    return dp, core, lax.axis_index("zl")


def cov_out_kernel(owners, counts, tokens, send, keep):
    dp, core, zl = counted()
    quarter = tokens.shape[0]
    live = counts[dp] - zl * quarter
    live = lax.broadcasted_iota(jnp.int32, (quarter, 256), 0) < live
    row = lax.broadcasted_iota(jnp.int32, (128, 128), 0)
    col = lax.broadcasted_iota(jnp.int32, (128, 128), 1)
    top = lax.broadcasted_iota(jnp.int32, (ROWS_EXTRA, 128), 0) == 0

    def block(x, zh, y, c):
        at = owners[((x * 2 + zh) * 4 + y) * 2 + c]
        return tokens[:, pl.ds(pl.multiple_of(at * 128, 128), 128)]

    def step(s, _):
        x, y = s // 4, s % 4
        for c, dst in ((core, keep), (1 - core, send)):
            full = jnp.concatenate([block(x, 0, y, c), block(x, 1, y, c)], axis=1)
            both = dot(jnp.where(live, full, jnp.zeros((), bf16)), full, 0, 0)
            first, second = both[:128, :128], both[128:, 128:]
            diag = jnp.sum(jnp.where(row == col, second, 0.0), axis=0, keepdims=True)
            dst[s, 0:ROWS_OUT] = jnp.where(row <= col, first, second).astype(dst.dtype)
            dst[s, ROWS_OUT:] = jnp.where(top, diag, 0.0).astype(dst.dtype)
        return 0

    lax.fori_loop(0, 16, step, 0, unroll=2)


def cov_in_rows(counts, tokens, send, keep, start):
    dp, core, _ = counted()
    first = core == 0
    live = lax.broadcasted_iota(jnp.int32, (tokens.shape[0], 256), 0) < counts[dp]
    for x in range(2):
        cols = slice((start + x) * 256, (start + x) * 256 + 256)
        some = jnp.where(live, tokens[:, cols], jnp.zeros((), bf16))
        part = dot(some, tokens[...], 0, 0)
        for zh in range(2):
            for y in range(4):
                at = (zh * 4 + y) * 32
                low, high = part[at : at + 16], part[at + 16 : at + 32]
                to = slice(zh * 16, zh * 16 + 16)
                keep[x * 4 + y, to] = jnp.where(first, low, high)
                send[x * 4 + y, to] = jnp.where(first, high, low).astype(bf16)


def cov_in_first_kernel(*refs):
    cov_in_rows(*refs, 0)


def cov_in_second_kernel(*refs):
    cov_in_rows(*refs, 2)


def pack_in_kernel(keep_one, recv_one, keep_two, recv_two, msg):
    def step(s, _):
        msg[s] = (keep_one[s] + recv_one[s].astype(f32)).astype(bf16)
        msg[8 + s] = (keep_two[s] + recv_two[s].astype(f32)).astype(bf16)
        return 0

    lax.fori_loop(0, 8, step, 0)


def pack_out_kernel(keep, recv, inner, other_inner, msg):
    total = inner[0:1] + other_inner[0:1]
    high = total.astype(bf16).astype(f32)
    rest = total - high
    middle = rest.astype(bf16).astype(f32)
    low = rest - middle
    row = lax.broadcasted_iota(jnp.int32, (ROWS_EXTRA, 128), 0)
    parts = jnp.where(
        row == 1, high, jnp.where(row == 2, middle, jnp.where(row == 3, low, 0.0))
    )

    def step(s, _):
        both = keep[s] + recv[s].astype(f32)
        msg[s, 0:ROWS_OUT] = both[0:ROWS_OUT].astype(bf16)
        msg[s, ROWS_OUT:] = (both[ROWS_OUT:] + parts).astype(bf16)
        return 0

    lax.fori_loop(0, 16, step, 0)


def slab_rows(core):
    zh = lax.axis_index("zh")
    for x in range(4):
        for y in range(4):
            for z in (zh, 1 - zh):
                slab = ((x * 2 + z) * 4 + y) * 2 + core
                yield pl.ds(pl.multiple_of(slab * 16, 16), 16)


def dot_slabs(left, slabs, core):
    picked = jnp.concatenate([left[rows, :] for rows in slab_rows(core)], axis=0)
    return dot(picked, slabs[...].reshape(512, 1024), 0, 0)


def rotate_kernel(slabs, grad, rotated):
    rotated[...] = dot_slabs(grad, slabs, lax.axis_index("core"))


def scale_kernel(slabs, grad, partial, q_out, values_in, values_out, back, inner_out):
    total = partial[...] + dot_slabs(grad, slabs, 1 - lax.axis_index("core"))
    q = q_out[...]
    spectral = dot(q, total.astype(bf16), 0, 0)
    scaled = (spectral / (values_in[...] * values_out[...] + damping)).astype(bf16)
    back_rot = dot(q, scaled, 1, 0).astype(bf16)
    back[...] = back_rot
    inner = jnp.sum(
        jnp.sum(back_rot.astype(f32) * total, axis=0, keepdims=True), axis=1, keepdims=True
    )
    inner_out[...] = jnp.broadcast_to(inner, (8, 128))


def finish_kernel(q_own, q_other, back, precond):
    core = lax.axis_index("core")
    for src, c in ((q_own, core), (q_other, 1 - core)):
        result = dot(src[...].reshape(512, 1024), back[...], 1, 1)
        for s, rows in enumerate(slab_rows(c)):
            precond[rows, :] = result[s * 16 : s * 16 + 16]


def clip_kernel(scalars, column, precond, cov_out, update):
    total = jnp.sum(column[...], axis=0)
    cov_out[0] = total[0:32] / scalars[0]
    rate = scalars[1]
    update[...] = jnp.minimum(1.0, jnp.sqrt(kl_clip / (rate * rate * total[32:33]))) * precond[...]


def on_chip(kernel, outs, flops, *args):
    whole = pl.BlockSpec(memory_space=pltpu.VMEM)
    size = sum(a.size * a.dtype.itemsize for a in args)
    return pl.pallas_call(
        kernel,
        in_specs=[whole if a.ndim > 1 else pl.BlockSpec(memory_space=pltpu.SMEM) for a in args],
        out_specs=[whole] * len(outs),
        out_shape=outs,
        compiler_params=pltpu.CompilerParams(vmem_limit_bytes=VMEM),
        cost_estimate=pl.CostEstimate(flops=flops, bytes_accessed=size, transcendentals=0),
        name=kernel.__name__[:-7],
    )(*args)


def total(msg, at, rows):
    out = msg[0, at : at + rows].astype(f32)
    for s in range(1, 16):
        out = out + msg[s, at : at + rows].astype(f32)
    return out


def unpack_in_kernel(msg, keep, send):
    first = lax.axis_index("zh") == 0
    pair = total(msg, 0, 32)
    low, high = pair[:16], pair[16:]
    keep[...] = jnp.where(first, low, high)
    send[...] = jnp.where(first, high, low)


def unpack_out_kernel(msg, column):
    folded = total(msg, 0, ROWS_OUT)
    extra = total(msg, ROWS_OUT, ROWS_EXTRA)
    turned = folded.T
    row = lax.broadcasted_iota(jnp.int32, (128, 128), 0)
    col = lax.broadcasted_iota(jnp.int32, (128, 128), 1)
    one = jnp.where(row <= col, folded, turned)
    two = jnp.where(row > col, folded, jnp.where(row == col, extra[0:1], turned))
    inner = jnp.broadcast_to(extra[1:2] + extra[2:3] + extra[3:4], (8, 128))
    for z in range(4):
        column[z, 0:32] = one[z * 32 : z * 32 + 32]
        column[4 + z, 0:32] = two[z * 32 : z * 32 + 32]
        column[z, 32:40] = inner
        column[4 + z, 32:40] = inner


def swap(array, axis):
    return lax.ppermute(array, axis, [(0, 1), (1, 0)])


def local(
    activations,
    output_grads,
    token_counts,
    owner_blocks,
    basis_in,
    basis_out,
    values_in,
    values_out,
    gradient,
    learning_rate,
):
    token_total = jnp.sum(token_counts).astype(f32)
    shape = jax.ShapeDtypeStruct
    mine = basis_in[0]
    slabs = jnp.concatenate([mine, swap(mine, "zh")], axis=0)
    half = [shape((8, 32, 1024), bf16), shape((8, 32, 1024), f32)]
    send_one, keep_one = on_chip(cov_in_first_kernel, half, 1 << 30, token_counts, activations)
    slabs, send_one, counts = lax.optimization_barrier((slabs, send_one, token_counts))
    q_own = lax.all_to_all(
        jnp.broadcast_to(slabs[None], (16,) + slabs.shape), PLANE, 0, 0, tiled=True
    )
    recv_one = swap(send_one, "core")
    send_two, keep_two = on_chip(cov_in_second_kernel, half, 1 << 30, counts, activations)
    recv_two = swap(send_two, "core")
    folded = (16, ROWS_OUT + ROWS_EXTRA, 128)
    send_out, keep_out = on_chip(
        cov_out_kernel,
        [shape(folded, bf16), shape(folded, f32)],
        1 << 30,
        owner_blocks,
        counts,
        output_grads,
    )
    recv_out = swap(send_out, "core")
    (msg_in,) = on_chip(
        pack_in_kernel,
        [shape((16, 32, 1024), bf16)],
        1024,
        keep_one,
        recv_one,
        keep_two,
        recv_two,
    )
    q_own, msg_in, keep_out = lax.optimization_barrier((q_own, msg_in, keep_out))
    got_in = lax.all_to_all(msg_in, PLANE, 0, 0, tiled=True)
    q_other = swap(q_own, "core")
    (partial,) = on_chip(rotate_kernel, [shape((128, 1024), f32)], 1024, q_own, gradient)
    back, inner = on_chip(
        scale_kernel,
        [shape((128, 1024), bf16), shape((8, 128), f32)],
        1024,
        q_other,
        gradient,
        partial,
        basis_out[0],
        values_in[None, :],
        values_out[:, None],
    )
    (precond,) = on_chip(finish_kernel, [shape((1024, 128), f32)], 1024, q_own, q_other, back)
    other_inner, precond = lax.optimization_barrier((swap(inner, "core"), precond))
    (msg_out,) = on_chip(
        pack_out_kernel,
        [shape(folded, bf16)],
        1024,
        keep_out,
        recv_out,
        inner,
        other_inner,
    )
    got_in, msg_out = lax.optimization_barrier((got_in, msg_out))
    got_out = lax.all_to_all(msg_out, PLANE, 0, 0, tiled=True)
    keep_slab, send_slab = on_chip(unpack_in_kernel, [shape((16, 1024), f32)] * 2, 1024, got_in)
    recv_slab = swap(send_slab, "zh")
    (column,) = on_chip(unpack_out_kernel, [shape((8, 40, 128), f32)], 1024, got_out)
    column, recv_slab = lax.optimization_barrier((column, recv_slab))
    column = lax.all_to_all(column, COLUMN, 0, 0, tiled=True)
    cov_in = ((keep_slab + recv_slab) / token_total)[None]
    cov_out, update = on_chip(
        clip_kernel,
        [shape((1, 32, 128), f32), shape((1024, 128), f32)],
        1 << 20,
        jnp.stack([token_total, learning_rate[0]]),
        column,
        precond,
    )
    return (cov_in, cov_out, update)


def solution(mesh):
    fine = Mesh(mesh.devices.reshape(SIZES), AXES)
    placed = (
        P(DP, "zl"),
        P(AXES, None),
        P(),
        P(),
        P("zl", DP, None),
        P(DP, None, None),
        P("zl"),
        P(DP),
        P("zl", DP),
        P(),
    )
    return jax.shard_map(
        local,
        mesh=fine,
        in_specs=placed,
        out_specs=(P("zl", DP, None), P(DP, "zl", None), P("zl", DP)),
        check_vma=False,
    )
```

```python
import jax
import jax.numpy as jnp
from jax import lax
from jax.experimental import pallas as pl
from jax.experimental.pallas import tpu as pltpu
from jax.sharding import Mesh, PartitionSpec as P

damping = 0.03
kl_clip = 0.001
f32 = jnp.float32
bf16 = jnp.bfloat16

AXES = ("x", "zh", "y", "core", "zl")
SIZES = (4, 2, 4, 2, 4)
DP = ("x", "zh", "y", "core")
PLANE = ("x", "y")
COLUMN = ("zh", "zl")
VMEM = 20 << 20

ROWS_OUT = 128
ROWS_EXTRA = 16


def dot(a, b, ca, cb):
    return lax.dot_general(a, b, (((ca,), (cb,)), ((), ())), preferred_element_type=f32)


def counted():
    core = lax.axis_index("core")
    dp = ((lax.axis_index("x") * 2 + lax.axis_index("zh")) * 4 + lax.axis_index("y")) * 2 + core
    return dp, core, lax.axis_index("zl")


def cov_out_kernel(owners, counts, tokens, send, keep):
    dp, core, zl = counted()
    quarter = tokens.shape[0]
    live = counts[dp] - zl * quarter
    live = lax.broadcasted_iota(jnp.int32, (quarter, 256), 0) < live
    row = lax.broadcasted_iota(jnp.int32, (128, 128), 0)
    col = lax.broadcasted_iota(jnp.int32, (128, 128), 1)
    top = lax.broadcasted_iota(jnp.int32, (ROWS_EXTRA, 128), 0) == 0

    def block(x, zh, y, c):
        at = owners[((x * 2 + zh) * 4 + y) * 2 + c]
        return tokens[:, pl.ds(pl.multiple_of(at * 128, 128), 128)]

    def step(s, _):
        x, y = s // 4, s % 4
        for c, dst in ((core, keep), (1 - core, send)):
            full = jnp.concatenate([block(x, 0, y, c), block(x, 1, y, c)], axis=1)
            both = dot(jnp.where(live, full, jnp.zeros((), bf16)), full, 0, 0)
            first, second = both[:128, :128], both[128:, 128:]
            diag = jnp.sum(jnp.where(row == col, second, 0.0), axis=0, keepdims=True)
            dst[s, 0:ROWS_OUT] = jnp.where(row <= col, first, second).astype(dst.dtype)
            dst[s, ROWS_OUT:] = jnp.where(top, diag, 0.0).astype(dst.dtype)
        return 0

    lax.fori_loop(0, 16, step, 0, unroll=2)


def cov_in_rows(counts, tokens, send, keep, start):
    dp, core, _ = counted()
    first = core == 0
    live = lax.broadcasted_iota(jnp.int32, (tokens.shape[0], 256), 0) < counts[dp]
    for x in range(send.shape[0] // 4):
        cols = slice((start + x) * 256, (start + x) * 256 + 256)
        some = jnp.where(live, tokens[:, cols], jnp.zeros((), bf16))
        part = dot(some, tokens[...], 0, 0)
        for zh in range(2):
            for y in range(4):
                at = (zh * 4 + y) * 32
                low, high = part[at : at + 16], part[at + 16 : at + 32]
                to = slice(zh * 16, zh * 16 + 16)
                keep[x * 4 + y, to] = jnp.where(first, low, high)
                send[x * 4 + y, to] = jnp.where(first, high, low).astype(bf16)


def cov_in_first_kernel(*refs):
    cov_in_rows(*refs, 0)


def cov_in_second_kernel(*refs):
    cov_in_rows(*refs, 3)


def pack_in_kernel(keep_one, recv_one, keep_two, recv_two, msg):
    def step(s, _):
        for at in range(3):
            to = at * 4 + s
            msg[to] = (keep_one[to] + recv_one[to].astype(f32)).astype(bf16)
        msg[12 + s] = (keep_two[s] + recv_two[s].astype(f32)).astype(bf16)
        return 0

    lax.fori_loop(0, 4, step, 0)


def pack_out_kernel(keep, recv, inner, other_inner, msg):
    total = inner[0:1] + other_inner[0:1]
    high = total.astype(bf16).astype(f32)
    rest = total - high
    middle = rest.astype(bf16).astype(f32)
    low = rest - middle
    row = lax.broadcasted_iota(jnp.int32, (ROWS_EXTRA, 128), 0)
    parts = jnp.where(
        row == 1, high, jnp.where(row == 2, middle, jnp.where(row == 3, low, 0.0))
    )

    def step(s, _):
        both = keep[s] + recv[s].astype(f32)
        msg[s, 0:ROWS_OUT] = both[0:ROWS_OUT].astype(bf16)
        msg[s, ROWS_OUT:] = (both[ROWS_OUT:] + parts).astype(bf16)
        return 0

    lax.fori_loop(0, 16, step, 0)


def slab_rows(core):
    zh = lax.axis_index("zh")
    for x in range(4):
        for y in range(4):
            for z in (zh, 1 - zh):
                slab = ((x * 2 + z) * 4 + y) * 2 + core
                yield pl.ds(pl.multiple_of(slab * 16, 16), 16)


def dot_slabs(left, slabs, core):
    picked = jnp.concatenate([left[rows, :] for rows in slab_rows(core)], axis=0)
    return dot(picked, slabs[...].reshape(512, 1024), 0, 0)


def rotate_kernel(slabs, grad, rotated):
    rotated[...] = dot_slabs(grad, slabs, lax.axis_index("core"))


def scale_kernel(slabs, grad, partial, q_out, values_in, values_out, back, inner_out):
    total = partial[...] + dot_slabs(grad, slabs, 1 - lax.axis_index("core"))
    q = q_out[...]
    spectral = dot(q, total.astype(bf16), 0, 0)
    scaled = (spectral / (values_in[...] * values_out[...] + damping)).astype(bf16)
    back_rot = dot(q, scaled, 1, 0).astype(bf16)
    back[...] = back_rot
    inner = jnp.sum(
        jnp.sum(back_rot.astype(f32) * total, axis=0, keepdims=True), axis=1, keepdims=True
    )
    inner_out[...] = jnp.broadcast_to(inner, (8, 128))


def finish_kernel(q_own, q_other, back, precond):
    core = lax.axis_index("core")
    for src, c in ((q_own, core), (q_other, 1 - core)):
        result = dot(src[...].reshape(512, 1024), back[...], 1, 1)
        for s, rows in enumerate(slab_rows(c)):
            precond[rows, :] = result[s * 16 : s * 16 + 16]


def clip_kernel(scalars, column, precond, cov_out, update):
    total = jnp.sum(column[...], axis=0)
    cov_out[0] = total[0:32] / scalars[0]
    rate = scalars[1]
    update[...] = jnp.minimum(1.0, jnp.sqrt(kl_clip / (rate * rate * total[32:33]))) * precond[...]


def on_chip(kernel, outs, flops, *args):
    whole = pl.BlockSpec(memory_space=pltpu.VMEM)
    size = sum(a.size * a.dtype.itemsize for a in args)
    return pl.pallas_call(
        kernel,
        in_specs=[whole if a.ndim > 1 else pl.BlockSpec(memory_space=pltpu.SMEM) for a in args],
        out_specs=[whole] * len(outs),
        out_shape=outs,
        compiler_params=pltpu.CompilerParams(vmem_limit_bytes=VMEM),
        cost_estimate=pl.CostEstimate(flops=flops, bytes_accessed=size, transcendentals=0),
        name=kernel.__name__[:-7],
    )(*args)


def total(msg, at, rows):
    out = msg[0, at : at + rows].astype(f32)
    for s in range(1, 16):
        out = out + msg[s, at : at + rows].astype(f32)
    return out


def unpack_in_kernel(msg, keep, send):
    first = lax.axis_index("zh") == 0
    pair = total(msg, 0, 32)
    low, high = pair[:16], pair[16:]
    keep[...] = jnp.where(first, low, high)
    send[...] = jnp.where(first, high, low)


def unpack_out_kernel(msg, column):
    folded = total(msg, 0, ROWS_OUT)
    extra = total(msg, ROWS_OUT, ROWS_EXTRA)
    turned = folded.T
    row = lax.broadcasted_iota(jnp.int32, (128, 128), 0)
    col = lax.broadcasted_iota(jnp.int32, (128, 128), 1)
    one = jnp.where(row <= col, folded, turned)
    two = jnp.where(row > col, folded, jnp.where(row == col, extra[0:1], turned))
    inner = jnp.broadcast_to(extra[1:2] + extra[2:3] + extra[3:4], (8, 128))
    for z in range(4):
        column[z, 0:32] = one[z * 32 : z * 32 + 32]
        column[4 + z, 0:32] = two[z * 32 : z * 32 + 32]
        column[z, 32:40] = inner
        column[4 + z, 32:40] = inner


def swap(array, axis):
    return lax.ppermute(array, axis, [(0, 1), (1, 0)])


def local(
    activations,
    output_grads,
    token_counts,
    owner_blocks,
    basis_in,
    basis_out,
    values_in,
    values_out,
    gradient,
    learning_rate,
):
    token_total = jnp.sum(token_counts).astype(f32)
    shape = jax.ShapeDtypeStruct
    mine = basis_in[0]
    slabs = jnp.concatenate([mine, swap(mine, "zh")], axis=0)
    most = [shape((12, 32, 1024), bf16), shape((12, 32, 1024), f32)]
    rest = [shape((4, 32, 1024), bf16), shape((4, 32, 1024), f32)]
    send_one, keep_one = on_chip(cov_in_first_kernel, most, 1 << 30, token_counts, activations)
    slabs, send_one, counts = lax.optimization_barrier((slabs, send_one, token_counts))
    q_own = lax.all_to_all(
        jnp.broadcast_to(slabs[None], (16,) + slabs.shape), PLANE, 0, 0, tiled=True
    )
    recv_one = swap(send_one, "core")
    send_two, keep_two = on_chip(cov_in_second_kernel, rest, 1 << 30, counts, activations)
    recv_two = swap(send_two, "core")
    folded = (16, ROWS_OUT + ROWS_EXTRA, 128)
    send_out, keep_out = on_chip(
        cov_out_kernel,
        [shape(folded, bf16), shape(folded, f32)],
        1 << 30,
        owner_blocks,
        counts,
        output_grads,
    )
    recv_out = swap(send_out, "core")
    (msg_in,) = on_chip(
        pack_in_kernel,
        [shape((16, 32, 1024), bf16)],
        1024,
        keep_one,
        recv_one,
        keep_two,
        recv_two,
    )
    q_own, msg_in, keep_out = lax.optimization_barrier((q_own, msg_in, keep_out))
    got_in = lax.all_to_all(msg_in, PLANE, 0, 0, tiled=True)
    q_other = swap(q_own, "core")
    (partial,) = on_chip(rotate_kernel, [shape((128, 1024), f32)], 1024, q_own, gradient)
    back, inner = on_chip(
        scale_kernel,
        [shape((128, 1024), bf16), shape((8, 128), f32)],
        1024,
        q_other,
        gradient,
        partial,
        basis_out[0],
        values_in[None, :],
        values_out[:, None],
    )
    (precond,) = on_chip(finish_kernel, [shape((1024, 128), f32)], 1024, q_own, q_other, back)
    other_inner, precond = lax.optimization_barrier((swap(inner, "core"), precond))
    (msg_out,) = on_chip(
        pack_out_kernel,
        [shape(folded, bf16)],
        1024,
        keep_out,
        recv_out,
        inner,
        other_inner,
    )
    got_in, msg_out = lax.optimization_barrier((got_in, msg_out))
    got_out = lax.all_to_all(msg_out, PLANE, 0, 0, tiled=True)
    keep_slab, send_slab = on_chip(unpack_in_kernel, [shape((16, 1024), f32)] * 2, 1024, got_in)
    recv_slab = swap(send_slab, "zh")
    (column,) = on_chip(unpack_out_kernel, [shape((8, 40, 128), f32)], 1024, got_out)
    column, recv_slab = lax.optimization_barrier((column, recv_slab))
    column = lax.all_to_all(column, COLUMN, 0, 0, tiled=True)
    cov_in = ((keep_slab + recv_slab) / token_total)[None]
    cov_out, update = on_chip(
        clip_kernel,
        [shape((1, 32, 128), f32), shape((1024, 128), f32)],
        1 << 20,
        jnp.stack([token_total, learning_rate[0]]),
        column,
        precond,
    )
    return (cov_in, cov_out, update)


def solution(mesh):
    fine = Mesh(mesh.devices.reshape(SIZES), AXES)
    placed = (
        P(DP, "zl"),
        P(AXES, None),
        P(),
        P(),
        P("zl", DP, None),
        P(DP, None, None),
        P("zl"),
        P(DP),
        P("zl", DP),
        P(),
    )
    return jax.shard_map(
        local,
        mesh=fine,
        in_specs=placed,
        out_specs=(P("zl", DP, None), P(DP, "zl", None), P("zl", DP)),
        check_vma=False,
    )
```

```python
import jax
import jax.numpy as jnp
from jax import lax
from jax.experimental import pallas as pl
from jax.experimental.pallas import tpu as pltpu
from jax.sharding import Mesh, PartitionSpec as P

damping = 0.03
kl_clip = 0.001
f32 = jnp.float32
bf16 = jnp.bfloat16

AXES = ("x", "zh", "y", "core", "zl")
SIZES = (4, 2, 4, 2, 4)
DP = ("x", "zh", "y", "core")
PLANE = ("x", "y")
COLUMN = ("zh", "zl")
VMEM = 20 << 20

ROWS_OUT = 128
ROWS_EXTRA = 16


def dot(a, b, ca, cb):
    return lax.dot_general(a, b, (((ca,), (cb,)), ((), ())), preferred_element_type=f32)


def counted():
    core = lax.axis_index("core")
    dp = ((lax.axis_index("x") * 2 + lax.axis_index("zh")) * 4 + lax.axis_index("y")) * 2 + core
    return dp, core, lax.axis_index("zl")


def cov_out_kernel(owners, counts, tokens, send, keep):
    dp, core, zl = counted()
    quarter = tokens.shape[0]
    live = counts[dp] - zl * quarter
    live = lax.broadcasted_iota(jnp.int32, (quarter, 256), 0) < live
    row = lax.broadcasted_iota(jnp.int32, (128, 128), 0)
    col = lax.broadcasted_iota(jnp.int32, (128, 128), 1)
    top = lax.broadcasted_iota(jnp.int32, (ROWS_EXTRA, 128), 0) == 0

    def block(x, zh, y, c):
        at = owners[((x * 2 + zh) * 4 + y) * 2 + c]
        return tokens[:, pl.ds(pl.multiple_of(at * 128, 128), 128)]

    def step(s, _):
        x, y = s // 4, s % 4
        for c, dst in ((core, keep), (1 - core, send)):
            full = jnp.concatenate([block(x, 0, y, c), block(x, 1, y, c)], axis=1)
            both = dot(jnp.where(live, full, jnp.zeros((), bf16)), full, 0, 0)
            first, second = both[:128, :128], both[128:, 128:]
            diag = jnp.sum(jnp.where(row == col, second, 0.0), axis=0, keepdims=True)
            dst[s, 0:ROWS_OUT] = jnp.where(row <= col, first, second).astype(dst.dtype)
            dst[s, ROWS_OUT:] = jnp.where(top, diag, 0.0).astype(dst.dtype)
        return 0

    lax.fori_loop(0, 16, step, 0, unroll=2)


def cov_in_rows(counts, tokens, send, keep, start):
    dp, core, _ = counted()
    first = core == 0
    live = lax.broadcasted_iota(jnp.int32, (tokens.shape[0], 256), 0) < counts[dp]
    for x in range(2):
        cols = slice((start + x) * 256, (start + x) * 256 + 256)
        some = jnp.where(live, tokens[:, cols], jnp.zeros((), bf16))
        part = dot(some, tokens[...], 0, 0)
        for zh in range(2):
            for y in range(4):
                at = (zh * 4 + y) * 32
                low, high = part[at : at + 16], part[at + 16 : at + 32]
                to = slice(zh * 16, zh * 16 + 16)
                keep[x * 4 + y, to] = jnp.where(first, low, high)
                send[x * 4 + y, to] = jnp.where(first, high, low).astype(bf16)


def cov_in_first_kernel(*refs):
    cov_in_rows(*refs, 0)


def cov_in_second_kernel(*refs):
    cov_in_rows(*refs, 2)


def pack_in_kernel(keep_one, recv_one, keep_two, recv_two, msg):
    def step(s, _):
        msg[s] = (keep_one[s] + recv_one[s].astype(f32)).astype(bf16)
        msg[8 + s] = (keep_two[s] + recv_two[s].astype(f32)).astype(bf16)
        return 0

    lax.fori_loop(0, 8, step, 0)


def pack_out_kernel(keep, recv, inner, other_inner, msg):
    total = inner[0:1] + other_inner[0:1]
    high = total.astype(bf16).astype(f32)
    rest = total - high
    middle = rest.astype(bf16).astype(f32)
    low = rest - middle
    row = lax.broadcasted_iota(jnp.int32, (ROWS_EXTRA, 128), 0)
    parts = jnp.where(
        row == 1, high, jnp.where(row == 2, middle, jnp.where(row == 3, low, 0.0))
    )

    def step(s, _):
        both = keep[s] + recv[s].astype(f32)
        msg[s, 0:ROWS_OUT] = both[0:ROWS_OUT].astype(bf16)
        msg[s, ROWS_OUT:] = (both[ROWS_OUT:] + parts).astype(bf16)
        return 0

    lax.fori_loop(0, 16, step, 0)


def slab_rows(core):
    zh = lax.axis_index("zh")
    for x in range(4):
        for y in range(4):
            for z in (zh, 1 - zh):
                slab = ((x * 2 + z) * 4 + y) * 2 + core
                yield pl.ds(pl.multiple_of(slab * 16, 16), 16)


def dot_slabs(left, slabs, core):
    picked = jnp.concatenate([left[rows, :] for rows in slab_rows(core)], axis=0)
    return dot(picked, slabs[...].reshape(512, 1024), 0, 0)


def rotate_kernel(slabs, grad, rotated):
    rotated[...] = dot_slabs(grad, slabs, lax.axis_index("core"))


def scale_kernel(slabs, grad, partial, q_out, values_in, values_out, back, inner_out):
    total = partial[...] + dot_slabs(grad, slabs, 1 - lax.axis_index("core"))
    q = q_out[...]
    spectral = dot(q, total.astype(bf16), 0, 0)
    scaled = (spectral / (values_in[...] * values_out[...] + damping)).astype(bf16)
    back_rot = dot(q, scaled, 1, 0).astype(bf16)
    back[...] = back_rot
    inner = jnp.sum(
        jnp.sum(back_rot.astype(f32) * total, axis=0, keepdims=True), axis=1, keepdims=True
    )
    inner_out[...] = jnp.broadcast_to(inner, (8, 128))


def finish_kernel(q_own, q_other, back, precond):
    core = lax.axis_index("core")
    for src, c in ((q_own, core), (q_other, 1 - core)):
        result = dot(src[...].reshape(512, 1024), back[...], 1, 1)
        for s, rows in enumerate(slab_rows(c)):
            precond[rows, :] = result[s * 16 : s * 16 + 16]


def clip_kernel(scalars, column, precond, cov_out, update, ready, sems):
    total = jnp.sum(column[...], axis=0)
    rate = scalars[1]
    factor = jnp.minimum(1.0, jnp.sqrt(kl_clip / (rate * rate * total[32:33])))
    copies = []
    for part in range(8):
        rows = pl.ds(part * 128, 128)
        ready[rows, :] = factor * precond[rows, :]
        copies.append(pltpu.make_async_copy(ready.at[rows], update.at[rows], sems.at[part]))
        copies[-1].start()
    cov_out[0] = total[0:32] / scalars[0]
    for copy in copies:
        copy.wait()


def clip(scalars, column, precond):
    whole = pl.BlockSpec(memory_space=pltpu.VMEM)
    return pl.pallas_call(
        clip_kernel,
        in_specs=[pl.BlockSpec(memory_space=pltpu.SMEM), whole, whole],
        out_specs=[whole, pl.BlockSpec(memory_space=pl.ANY)],
        out_shape=[jax.ShapeDtypeStruct((1, 32, 128), f32), jax.ShapeDtypeStruct((1024, 128), f32)],
        scratch_shapes=[pltpu.VMEM((1024, 128), f32), pltpu.SemaphoreType.DMA((8,))],
        compiler_params=pltpu.CompilerParams(vmem_limit_bytes=VMEM),
        cost_estimate=pl.CostEstimate(flops=1024, bytes_accessed=1024, transcendentals=0),
        name="clip",
    )(scalars, column, precond)


def on_chip(kernel, outs, flops, *args):
    whole = pl.BlockSpec(memory_space=pltpu.VMEM)
    size = sum(a.size * a.dtype.itemsize for a in args)
    return pl.pallas_call(
        kernel,
        in_specs=[whole if a.ndim > 1 else pl.BlockSpec(memory_space=pltpu.SMEM) for a in args],
        out_specs=[whole] * len(outs),
        out_shape=outs,
        compiler_params=pltpu.CompilerParams(vmem_limit_bytes=VMEM),
        cost_estimate=pl.CostEstimate(flops=flops, bytes_accessed=size, transcendentals=0),
        name=kernel.__name__[:-7],
    )(*args)


def total(msg, at, rows):
    out = msg[0, at : at + rows].astype(f32)
    for s in range(1, 16):
        out = out + msg[s, at : at + rows].astype(f32)
    return out


def unpack_in_kernel(msg, keep, send):
    first = lax.axis_index("zh") == 0
    pair = total(msg, 0, 32)
    low, high = pair[:16], pair[16:]
    keep[...] = jnp.where(first, low, high)
    send[...] = jnp.where(first, high, low)


def unpack_out_kernel(msg, column):
    folded = total(msg, 0, ROWS_OUT)
    extra = total(msg, ROWS_OUT, ROWS_EXTRA)
    turned = folded.T
    row = lax.broadcasted_iota(jnp.int32, (128, 128), 0)
    col = lax.broadcasted_iota(jnp.int32, (128, 128), 1)
    one = jnp.where(row <= col, folded, turned)
    two = jnp.where(row > col, folded, jnp.where(row == col, extra[0:1], turned))
    inner = jnp.broadcast_to(extra[1:2] + extra[2:3] + extra[3:4], (8, 128))
    for z in range(4):
        column[z, 0:32] = one[z * 32 : z * 32 + 32]
        column[4 + z, 0:32] = two[z * 32 : z * 32 + 32]
        column[z, 32:40] = inner
        column[4 + z, 32:40] = inner


def swap(array, axis):
    return lax.ppermute(array, axis, [(0, 1), (1, 0)])


def local(
    activations,
    output_grads,
    token_counts,
    owner_blocks,
    basis_in,
    basis_out,
    values_in,
    values_out,
    gradient,
    learning_rate,
):
    token_total = jnp.sum(token_counts).astype(f32)
    shape = jax.ShapeDtypeStruct
    mine = basis_in[0]
    slabs = jnp.concatenate([mine, swap(mine, "zh")], axis=0)
    half = [shape((8, 32, 1024), bf16), shape((8, 32, 1024), f32)]
    send_one, keep_one = on_chip(cov_in_first_kernel, half, 1 << 30, token_counts, activations)
    slabs, send_one, counts = lax.optimization_barrier((slabs, send_one, token_counts))
    q_own = lax.all_to_all(
        jnp.broadcast_to(slabs[None], (16,) + slabs.shape), PLANE, 0, 0, tiled=True
    )
    recv_one = swap(send_one, "core")
    send_two, keep_two = on_chip(cov_in_second_kernel, half, 1 << 30, counts, activations)
    recv_two = swap(send_two, "core")
    folded = (16, ROWS_OUT + ROWS_EXTRA, 128)
    send_out, keep_out = on_chip(
        cov_out_kernel,
        [shape(folded, bf16), shape(folded, f32)],
        1 << 30,
        owner_blocks,
        counts,
        output_grads,
    )
    recv_out = swap(send_out, "core")
    (msg_in,) = on_chip(
        pack_in_kernel,
        [shape((16, 32, 1024), bf16)],
        1024,
        keep_one,
        recv_one,
        keep_two,
        recv_two,
    )
    q_own, msg_in, keep_out = lax.optimization_barrier((q_own, msg_in, keep_out))
    got_in = lax.all_to_all(msg_in, PLANE, 0, 0, tiled=True)
    q_other = swap(q_own, "core")
    (partial,) = on_chip(rotate_kernel, [shape((128, 1024), f32)], 1024, q_own, gradient)
    back, inner = on_chip(
        scale_kernel,
        [shape((128, 1024), bf16), shape((8, 128), f32)],
        1024,
        q_other,
        gradient,
        partial,
        basis_out[0],
        values_in[None, :],
        values_out[:, None],
    )
    (precond,) = on_chip(finish_kernel, [shape((1024, 128), f32)], 1024, q_own, q_other, back)
    other_inner, precond = lax.optimization_barrier((swap(inner, "core"), precond))
    (msg_out,) = on_chip(
        pack_out_kernel,
        [shape(folded, bf16)],
        1024,
        keep_out,
        recv_out,
        inner,
        other_inner,
    )
    got_in, msg_out = lax.optimization_barrier((got_in, msg_out))
    got_out = lax.all_to_all(msg_out, PLANE, 0, 0, tiled=True)
    keep_slab, send_slab = on_chip(unpack_in_kernel, [shape((16, 1024), f32)] * 2, 1024, got_in)
    recv_slab = swap(send_slab, "zh")
    (column,) = on_chip(unpack_out_kernel, [shape((8, 40, 128), f32)], 1024, got_out)
    column, recv_slab = lax.optimization_barrier((column, recv_slab))
    column = lax.all_to_all(column, COLUMN, 0, 0, tiled=True)
    cov_in = ((keep_slab + recv_slab) / token_total)[None]
    cov_out, update = clip(jnp.stack([token_total, learning_rate[0]]), column, precond)
    return (cov_in, cov_out, update)


def solution(mesh):
    fine = Mesh(mesh.devices.reshape(SIZES), AXES)
    placed = (
        P(DP, "zl"),
        P(AXES, None),
        P(),
        P(),
        P("zl", DP, None),
        P(DP, None, None),
        P("zl"),
        P(DP),
        P("zl", DP),
        P(),
    )
    return jax.shard_map(
        local,
        mesh=fine,
        in_specs=placed,
        out_specs=(P("zl", DP, None), P(DP, "zl", None), P("zl", DP)),
        check_vma=False,
    )
```
